128 devices in a mesh: lon: 16 (over z, y_hi, core), lat: 8 (over y_lo, x).
Axes of the slice: x: 4, y: 4 (y_hi: 2, y_lo: 2; y = y_hi * 2 + y_lo), z: 4, core: 2. Of those that a mesh axis runs over, the one named last changes fastest.
Arguments:
- ocean_state: bfloat16 [4, 75, 64, 4096], P(None, None, 'lat', 'lon'), may hold values from -6 to 6
- sea_mask: int32 [75, 64, 4096], P(None, 'lat', 'lon'), may hold values from 0 to 1
- fold_partner: int32 [4096], P('lon'), may hold values from 0 to 4095, as said below
- first_kernel: bfloat16 [9, 256, 75], replicated, may hold values from -0.25 to 0.25
- first_bias: float32 [256], replicated, may hold values from -3 to 3
- second_kernel: bfloat16 [9, 256, 256], replicated, may hold values from -0.125 to 0.125
- second_bias: float32 [256], replicated, may hold values from -3 to 3
Outputs:
- tendency: bfloat16 [4, 256, 64, 4096], P(None, None, 'lat', 'lon')
The draws below stay inside these ranges and needn't reach their ends.
Inputs may be any that keep to these rules, and one draw needn't show every extreme that they name: sea_mask is 0 or 1 and never rises with level at a cell; fold_partner[j] = (s - j) mod 4096 for one whole number s.
All inputs are finite; a program needn't handle non-finite values.
Results may differ from the reference program's by a relative error of at most 0.0039.
Values may be sent and summed in bfloat16 or wider, within the bound.
A program may use at most 192 MiB of HBM per device.

```python
import jax
import jax.numpy as jnp
from jax import lax

CIN = 75
HID = 256
SAMPLES = 4
NROWS = 64
NCOLS = 4096


def draw_sea_mask(key, part):
    key = jax.random.fold_in(key, 1)
    depth_level = jax.random.randint(key, (NROWS, NCOLS), -(CIN // 4), CIN + 1)
    levels = jnp.arange(CIN, dtype=jnp.int32)
    return (levels[:, None, None] < depth_level[None]).astype(jnp.int32)


def draw_fold_partner(key, part):
    key = jax.random.fold_in(key, 2)
    offset = jax.random.randint(key, (), 0, NCOLS)
    columns = jnp.arange(NCOLS, dtype=jnp.int32)
    return ((offset - columns) % NCOLS).astype(jnp.int32)


def block_scale(stream_key, dims, shards, low, top_value):
    def one(dim, parts):
        draws = jax.random.uniform(jax.random.fold_in(jax.random.fold_in(stream_key, 6), dim), (parts,), jnp.float32, low / len(shards), top_value / len(shards))
        return jnp.repeat(jnp.exp(draws), dims[dim] // parts).reshape((-1,) + (1,) * (len(dims) - dim - 1))

    factor_of = one(*shards[0])
    for cut in shards[1:]:
        factor_of = factor_of * one(*cut)
    return factor_of


def centred(rng, dims, deviation, bound, pieces=(), kind=jnp.bfloat16):
    entries = deviation * jax.random.normal(rng, dims, jnp.float32)
    if pieces:
        entries = entries * block_scale(rng, dims, pieces, -0.22, 0.18)
    return jnp.clip(entries, -bound, bound).astype(kind)


def setup_inputs(seed: int = 0) -> dict:
    streams_of = jax.random.split(jax.random.key(seed), 8)
    ocean_state = centred(streams_of[0], (SAMPLES, CIN, NROWS, NCOLS), 1.0, 6.0, ((2, 8), (3, 16)))
    sea_mask = draw_sea_mask(jax.random.fold_in(streams_of[7], 71), 0)
    fold_partner = draw_fold_partner(jax.random.fold_in(streams_of[7], 71), 0)
    first_kernel = centred(streams_of[3], (9, HID, CIN), (9 * CIN) ** -0.5, 0.25)
    first_bias = centred(streams_of[4], (HID,), 0.5, 3.0, (), jnp.float32)
    second_kernel = centred(streams_of[5], (9, HID, HID), (9 * HID) ** -0.5, 0.125)
    second_bias = centred(streams_of[6], (HID,), 0.5, 3.0, (), jnp.float32)
    return {"ocean_state": ocean_state, "sea_mask": sea_mask, "fold_partner": fold_partner, "first_kernel": first_kernel, "first_bias": first_bias, "second_kernel": second_kernel, "second_bias": second_bias}


def pad_field(field, fold_partner):
    ghost_row = jnp.take(field[:, :, -1, :], fold_partner, axis=2)
    zero_row = jnp.zeros_like(ghost_row)
    row_padded = jnp.concatenate([zero_row[:, :, None, :], field, ghost_row[:, :, None, :]], axis=2)
    return jnp.concatenate([row_padded[..., -1:], row_padded, row_padded[..., :1]], axis=3)


def convolve(padded, kernel):
    def one_sample(sample):
        row_count = sample.shape[1] - 2
        col_count = sample.shape[2] - 2
        running = jnp.zeros((kernel.shape[1], row_count, col_count), jnp.float32)
        for tap_row in range(3):
            for tap_col in range(3):
                window = sample[:, tap_row:tap_row + row_count, tap_col:tap_col + col_count].astype(jnp.float32)
                running = running + jnp.einsum('oc,crw->orw', kernel[3 * tap_row + tap_col].astype(jnp.float32), window)
        return running

    return lax.map(one_sample, padded)


def reference(ocean_state, sea_mask, fold_partner, first_kernel, first_bias, second_kernel, second_bias):
    masked = ocean_state * sea_mask.astype(jnp.bfloat16)[None]
    surface = sea_mask[0].astype(jnp.float32)
    first_out = convolve(pad_field(masked, fold_partner), first_kernel) + first_bias[None, :, None, None]
    hidden = (jax.nn.gelu(first_out) * surface).astype(jnp.bfloat16)
    second_out = convolve(pad_field(hidden, fold_partner), second_kernel) + second_bias[None, :, None, None]
    return (second_out * surface).astype(jnp.bfloat16)
```

```python
import functools

import jax
import jax.numpy as jnp
from jax import lax
from jax.experimental import pallas as pl
from jax.experimental.pallas import tpu as pltpu
from jax.sharding import PartitionSpec as P

F32 = jnp.float32
BF16 = jnp.bfloat16
MESH = pl.DeviceIdType.MESH
VMEM = pl.BlockSpec(memory_space=pltpu.VMEM)
SMEM = pl.BlockSpec(memory_space=pltpu.SMEM)

SAMPLES, CIN, ROWS, COLS, HID = 4, 75, 8, 256, 256
CPAD = 80
WIDE = SAMPLES * COLS
XROWS = ROWS + 4
HROWS = ROWS + 2
NLON, NLAT = 16, 8
LIMIT = 60 * 1024 * 1024


def lanes_of(shape):
    return lax.broadcasted_iota(jnp.int32, shape, len(shape) - 1)


def edge_pairs(x_ref, rows, left, right):
    pair = lax.shift_right_logical(lanes_of((CPAD, 128)), 1)
    for r in rows:
        for s in range(SAMPLES):
            row = x_ref[r, :, s * COLS : (s + 1) * COLS].astype(F32)
            at = 8 * r + 2 * s
            here = pair == at // 2
            left = jnp.where(here, pltpu.roll(row[:, :128], at, 1), left)
            right = jnp.where(here, pltpu.roll(row[:, 128:], (at + 2) % 128, 1), right)
    return left, right


def prepare(state_ref, mask_ref, x_ref, t_ref):
    for s in range(SAMPLES):
        for h in range(2):
            cut = slice(h * 128, (h + 1) * 128)
            t_ref[s, h, CIN * ROWS : (CIN + 1) * ROWS, :] = mask_ref[0, :, cut].astype(F32)
            t_ref[s, h, (CIN + 1) * ROWS :, :] = jnp.zeros(((CPAD - CIN - 1) * ROWS, 128), F32)
            masked = state_ref[s, :, :, cut].astype(F32) * mask_ref[:, :, cut].astype(F32)
            t_ref[s, h, : CIN * ROWS, :] = masked.reshape(CIN * ROWS, 128)
            for r in range(ROWS):
                at = s * COLS + h * 128
                x_ref[r + 2, :, at : at + 128] = t_ref[s, h, pl.ds(r, CPAD, stride=ROWS), :].astype(BF16)


def piece(i):
    return i // 8, (i // 2) % 4, i % 2


HALF = ((0, 48), (48, 32))


def exchange_kernel(
    state_ref, mask_ref, fold_ref, x_out, e_out,
    x_ref, t_ref, sp_ref, lp_ref, rp_ref, a_ref, y0_ref, y1_ref, s_ref, sp2_ref, p2_ref,
    row_send, row_recv, edge_send, edge_recv, f1_send, f1_recv, f2_send, f2_recv, f3_send, f3_recv,
):
    lon = lax.axis_index("lon")
    lat = lax.axis_index("lat")
    right, left = lax.rem(lon + 1, NLON), lax.rem(lon + NLON - 1, NLON)
    top = lat == NLAT - 1
    has = {-1: lat > 0, 0: None, 1: lat < NLAT - 1}

    def when(flag, fn):
        if flag is None:
            fn()
        else:
            pl.when(flag)(fn)

    barrier = pltpu.get_barrier_semaphore()

    def greet(at_lat, at_lon):
        pl.semaphore_signal(barrier, inc=1, device_id={"lat": at_lat, "lon": at_lon}, device_id_type=MESH)

    for d in (-1, 0, 1):
        def hello(d=d):
            if d:
                greet(lat + d, lon)
            greet(lat + d, left)
            greet(lat + d, right)
        when(has[d], hello)

    @pl.when(top)
    def _():
        for k in range(2, NLON - 1):
            greet(lat, lax.rem(lon + k, NLON))

    prepare(state_ref, mask_ref, x_ref, t_ref)
    zero = jnp.zeros((CPAD, 128), F32)
    own_left, own_right = edge_pairs(x_ref, range(2, 2 + ROWS), zero, zero)
    sp_ref[0] = own_left.astype(BF16)
    sp_ref[1] = own_right.astype(BF16)

    @pl.when(lat == 0)
    def _():
        x_ref[0:2] = jnp.zeros((2, CPAD, WIDE), BF16)
        lp_ref[0] = jnp.zeros((CPAD, 128), BF16)
        rp_ref[0] = jnp.zeros((CPAD, 128), BF16)

    @pl.when(jnp.logical_and(lat > 0, lat < NLAT - 1))
    def _():
        pl.semaphore_wait(barrier, 8)

    @pl.when(lat == 0)
    def _():
        pl.semaphore_wait(barrier, 5)

    @pl.when(top)
    def _():
        pl.semaphore_wait(barrier, 18)

    def to(src, dst, send, recv, at_lat, at_lon):
        return pltpu.make_async_remote_copy(
            src_ref=src, dst_ref=dst, send_sem=send, recv_sem=recv,
            device_id={"lat": at_lat, "lon": at_lon}, device_id_type=MESH,
        )

    def first_copy(i):
        row, s, half = piece(i)
        at, n = HALF[half]
        return to(
            x_ref.at[9 - row, pl.ds(at, n), pl.ds(s * COLS, COLS)], a_ref.at[lon, pl.ds(0, n)],
            f1_send.at[i], f1_recv.at[lon], lat, i,
        )

    my_row, my_s, my_half = piece(lon)

    def second_copy(d, half):
        at, n = HALF[half]
        return to(
            s_ref.at[d, pl.ds(0, n)],
            x_ref.at[10 + my_row, pl.ds(at, n), pl.ds(pl.multiple_of(my_s * COLS, COLS), COLS)],
            f2_send.at[d], f2_recv.at[lon], lat, d,
        )

    up = to(x_ref.at[pl.ds(8, 2)], x_ref.at[pl.ds(0, 2)], row_send.at[0], row_recv.at[0], lat + 1, lon)
    down = to(x_ref.at[pl.ds(2, 2)], x_ref.at[pl.ds(10, 2)], row_send.at[1], row_recv.at[1], lat - 1, lon)
    edge = {}
    for d in (-1, 0, 1):
        edge[d] = (
            to(sp_ref.at[0], rp_ref.at[1 - d], edge_send.at[d + 1], edge_recv.at[1 - d], lat + d, left),
            to(sp_ref.at[1], lp_ref.at[1 - d], edge_send.at[d + 4], edge_recv.at[4 - d], lat + d, right),
        )

    @pl.when(top)
    def _():
        for i in range(NLON):
            pl.when(i != lon)(lambda i=i: first_copy(i).start())

    for d in (-1, 0, 1):
        def go(d=d):
            edge[d][0].start()
            edge[d][1].start()
        when(has[d], go)
    pl.when(has[1])(lambda: up.start())
    pl.when(has[-1])(lambda: down.start())

    @pl.when(top)
    def _():
        for half in (0, 1):
            at, n = HALF[half]

            @pl.when(my_half == half)
            def _():
                mine = x_ref.at[9 - my_row, pl.ds(at, n), pl.ds(pl.multiple_of(my_s * COLS, COLS), COLS)]
                a_ref[lon, 0:n] = mine[...]
                if n < 48:
                    a_ref[:, n:] = jnp.zeros((NLON, 48 - n, COLS), BF16)
                for e in range(NLON):
                    def arrive(e=e):
                        to(a_ref.at[e, pl.ds(0, n)], a_ref.at[e, pl.ds(0, n)], f1_send.at[e], f1_recv.at[e], lat, e).wait_recv()
                    pl.when(e != lon)(arrive)

        start = fold_ref[0]
        turn = jnp.bitwise_and(start, COLS - 1)
        block = lax.shift_right_logical(start, 8)
        both = lax.broadcasted_iota(jnp.int32, (COLS, COLS), 0) + lax.broadcasted_iota(jnp.int32, (COLS, COLS), 1)
        pieces = a_ref[...].reshape(NLON * 48, COLS)
        for y_ref, target in ((y0_ref, turn), (y1_ref, turn + COLS)):
            choose = jnp.where(both == target, 1.0, 0.0).astype(BF16)
            y_ref[...] = jnp.dot(pieces, choose, preferred_element_type=F32).astype(BF16).reshape(NLON, 48, COLS)
        for d in range(NLON):
            b = jnp.bitwise_and(block + lon - d, NLON - 1)
            s_ref[d] = y0_ref[b] + y1_ref[jnp.bitwise_and(b + NLON - 1, NLON - 1)]
        for half in (0, 1):
            at, n = HALF[half]

            @pl.when(my_half == half)
            def _():
                for d in range(NLON):
                    pl.when(d != lon)(lambda d=d: second_copy(d, half).start())
                x_ref[10 + my_row, at : at + n, pl.ds(pl.multiple_of(my_s * COLS, COLS), COLS)] = s_ref[lon, 0:n]

    for d in (-1, 0, 1):
        def got(d=d):
            edge[-d][0].wait_recv()
            edge[-d][1].wait_recv()
        when(has[d], got)
    pl.when(has[1])(lambda: down.wait_recv())
    pl.when(has[-1])(lambda: up.wait_recv())

    @pl.when(top)
    def _():
        for e in range(NLON):
            row, s, half = piece(e)
            at, n = HALF[half]
            def arrive(e=e, row=row, s=s, at=at, n=n):
                there = x_ref.at[10 + row, pl.ds(at, n), pl.ds(s * COLS, COLS)]
                to(there, there, f2_send.at[e], f2_recv.at[e], lat, e).wait_recv()
            pl.when(e != lon)(arrive)

    far_left, far_right = edge_pairs(x_ref, (0, 1, 10, 11), own_left, own_right)

    @pl.when(top)
    def _():
        sp2_ref[0] = far_left.astype(BF16)
        sp2_ref[1] = far_right.astype(BF16)
        third = [
            to(sp2_ref.at[0], p2_ref.at[0], f3_send.at[0], f3_recv.at[0], lat, left),
            to(sp2_ref.at[1], p2_ref.at[1], f3_send.at[1], f3_recv.at[1], lat, right),
        ]
        for copy in third:
            copy.start()
        for copy in third:
            copy.wait()
        rp_ref[2] = pltpu.roll(p2_ref[0].astype(F32), 64, 1).astype(BF16)
        lp_ref[2] = pltpu.roll(p2_ref[1].astype(F32), 64, 1).astype(BF16)

    lane = lanes_of((CPAD, 128))

    def joined(ref):
        below = pltpu.roll(ref[0].astype(F32), 64, 1)
        above = pltpu.roll(ref[2].astype(F32), 64, 1)
        return jnp.where(lane < 16, below, jnp.where(lane < 80, ref[1].astype(F32), above))

    before, after = joined(lp_ref), joined(rp_ref)
    even = jnp.bitwise_and(lane, 1) == 0
    e_out[0] = jnp.where(even, before, far_right).astype(BF16)
    e_out[1] = jnp.where(even, pltpu.roll(before, 127, 1), pltpu.roll(after, 1, 1)).astype(BF16)
    e_out[2] = jnp.where(even, far_left, after).astype(BF16)
    x_out[...] = x_ref[...]

    pl.when(has[1])(lambda: up.wait_send())
    pl.when(has[-1])(lambda: down.wait_send())
    for d in (-1, 0, 1):
        def sent(d=d):
            edge[d][0].wait_send()
            edge[d][1].wait_send()
        when(has[d], sent)

    @pl.when(top)
    def _():
        for i in range(NLON):
            pl.when(i != lon)(lambda i=i: first_copy(i).wait_send())
        for half in (0, 1):
            @pl.when(my_half == half)
            def _():
                for d in range(NLON):
                    pl.when(d != lon)(lambda d=d: second_copy(d, half).wait_send())


def exchange(state, mask, fold):
    dma = pltpu.SemaphoreType.DMA
    return pl.pallas_call(
        exchange_kernel,
        out_shape=(
            jax.ShapeDtypeStruct((XROWS, CPAD, WIDE), BF16),
            jax.ShapeDtypeStruct((3, CPAD, 128), BF16),
        ),
        in_specs=[VMEM, VMEM, SMEM],
        out_specs=(VMEM, VMEM),
        scratch_shapes=[
            pltpu.VMEM((XROWS, CPAD, WIDE), BF16),
            pltpu.VMEM((SAMPLES, 2, CPAD * ROWS, 128), F32),
            pltpu.VMEM((2, CPAD, 128), BF16),
            pltpu.VMEM((3, CPAD, 128), BF16),
            pltpu.VMEM((3, CPAD, 128), BF16),
            pltpu.VMEM((NLON, 48, COLS), BF16),
            pltpu.VMEM((NLON, 48, COLS), BF16),
            pltpu.VMEM((NLON, 48, COLS), BF16),
            pltpu.VMEM((NLON, 48, COLS), BF16),
            pltpu.VMEM((2, CPAD, 128), BF16),
            pltpu.VMEM((2, CPAD, 128), BF16),
            dma((2,)), dma((2,)), dma((6,)), dma((6,)),
            dma((NLON,)), dma((NLON,)), dma((NLON,)), dma((NLON,)), dma((2,)), dma((2,)),
        ],
        compiler_params=pltpu.CompilerParams(collective_id=0, has_side_effects=True, vmem_limit_bytes=LIMIT),
    )(state, mask, fold)


def shift_rows(x_ref, e_ref, xb_ref, rows):
    lane = jnp.bitwise_and(lanes_of((CPAD, WIDE)), COLS - 1)
    for r in rows:
        row = x_ref[r].astype(F32)
        xb_ref[r, CPAD : 2 * CPAD, :] = x_ref[r]
        lower, upper = pltpu.roll(row, 1, 1), pltpu.roll(row, WIDE - 1, 1)
        mid = e_ref[1].astype(F32)
        firsts, lasts = [], []
        for s in range(SAMPLES):
            at = 8 * r + 2 * s
            firsts += [pltpu.roll(mid, (128 - at) % 128, 1), mid]
            lasts += [mid, pltpu.roll(mid, (127 - at - 1) % 128, 1)]
        xb_ref[r, :CPAD, :] = jnp.where(lane == 0, jnp.concatenate(firsts, 1), lower).astype(BF16)
        xb_ref[r, 2 * CPAD :, :] = jnp.where(lane == COLS - 1, jnp.concatenate(lasts, 1), upper).astype(BF16)


def gelu(x):
    return 0.5 * x * (1.0 + jnp.tanh(0.7978845608028654 * (x + 0.044715 * (x * x * x))))


def edge_hidden(e_ref, k1_ref, bias, top):
    taps = []
    for a in range(3):
        for b in range(3):
            taps.append(pltpu.roll(e_ref[b].astype(F32), (128 - 8 * a) % 128, 1))
    xe = jnp.concatenate(taps, 0).astype(BF16)
    plain = jnp.dot(k1_ref[0], xe, preferred_element_type=F32)
    turned = jnp.dot(k1_ref[1], xe, preferred_element_type=F32)
    lane = lanes_of((HID, 128))
    ghost = lane >= jnp.where(top, 72, 128)
    out = jnp.where(ghost, turned, plain) + bias
    surface = taps[4][CIN : CIN + 1, :]
    return gelu(out) * surface


def hidden_rows(x_ref, xb_ref, hb_ref, he_ref, k1_ref, bias, top, r):
    which = jnp.where(top, 1, 0) if r == HROWS - 1 else 0
    kernel = k1_ref[which]
    lane = jnp.bitwise_and(lanes_of((HID, 2 * COLS)), COLS - 1)
    taps = xb_ref[r : r + 3].reshape(9 * CPAD, WIDE)
    for pair in range(2):
        cut = slice(pair * 2 * COLS, (pair + 1) * 2 * COLS)
        out = jnp.dot(kernel, taps[:, cut], preferred_element_type=F32)
        surface = x_ref[r + 1, CIN - 11 : CPAD, cut].astype(F32)[11:12]
        out = gelu(out + jnp.concatenate([bias] * 4, 1)) * surface
        hb_ref[r, HID : 2 * HID, cut] = out.astype(BF16)
        lower, upper = pltpu.roll(out, 1, 1), pltpu.roll(out, 2 * COLS - 1, 1)
        firsts, lasts = [], []
        edge = he_ref[...]
        for s in (2 * pair, 2 * pair + 1):
            at = 8 * r + 2 * s
            firsts += [pltpu.roll(edge, (128 - at) % 128, 1), edge]
            lasts += [edge, pltpu.roll(edge, (127 - at - 1) % 128, 1)]
        hb_ref[r, :HID, cut] = jnp.where(lane == 0, jnp.concatenate(firsts, 1), lower).astype(BF16)
        hb_ref[r, 2 * HID :, cut] = jnp.where(lane == COLS - 1, jnp.concatenate(lasts, 1), upper).astype(BF16)


def output_rows(x_ref, hb_ref, k2_ref, of_ref, bias, r):
    kernel = jnp.concatenate([k2_ref[t] for t in range(9)], 1)
    taps = hb_ref[r : r + 3].reshape(9 * HID, WIDE)
    for pair in range(2):
        cut = slice(pair * 2 * COLS, (pair + 1) * 2 * COLS)
        out = jnp.dot(kernel, taps[:, cut], preferred_element_type=F32)
        surface = x_ref[r + 2, CIN - 11 : CPAD, cut].astype(F32)[11:12]
        out = (out + jnp.concatenate([bias] * 4, 1)) * surface
        for s in range(2):
            for h in range(2):
                at = s * COLS + h * 128
                of_ref[2 * pair + s, h, pl.ds(r, HID, stride=ROWS), :] = out[:, at : at + 128]


def wide_bias(ref):
    return jnp.transpose(jnp.broadcast_to(ref[...], (128, HID)))


def compute_kernel(x_ref, e_ref, k1_ref, b1_ref, k2_ref, b2_ref, out_ref, xb_ref, hb_ref, he_ref, of_ref):
    top = lax.axis_index("lat") == NLAT - 1
    bias1, bias2 = wide_bias(b1_ref), wide_bias(b2_ref)
    he_ref[...] = edge_hidden(e_ref, k1_ref, bias1, top)
    shift_rows(x_ref, e_ref, xb_ref, range(XROWS))
    for r in range(HROWS):
        hidden_rows(x_ref, xb_ref, hb_ref, he_ref, k1_ref, bias1, top, r)
    for r in range(ROWS):
        output_rows(x_ref, hb_ref, k2_ref, of_ref, bias2, r)
    for s in range(SAMPLES):
        for h in range(2):
            out_ref[s, :, :, h * 128 : (h + 1) * 128] = of_ref[s, h].reshape(HID, ROWS, 128).astype(BF16)


def compute(x, e, k1, b1, k2, b2):
    return pl.pallas_call(
        compute_kernel,
        out_shape=jax.ShapeDtypeStruct((SAMPLES, HID, ROWS, COLS), BF16),
        in_specs=[VMEM] * 6,
        out_specs=VMEM,
        scratch_shapes=[
            pltpu.VMEM((XROWS, 3 * CPAD, WIDE), BF16),
            pltpu.VMEM((HROWS, 3 * HID, WIDE), BF16),
            pltpu.VMEM((HID, 128), F32),
            pltpu.VMEM((SAMPLES, 2, HID * ROWS, 128), F32),
        ],
        compiler_params=pltpu.CompilerParams(vmem_limit_bytes=LIMIT),
    )(x, e, k1, b1, k2, b2)


def on_device(state, mask, fold, first_kernel, first_bias, second_kernel, second_bias):
    taps = jnp.pad(first_kernel, ((0, 0), (0, 0), (0, CPAD - CIN)))
    both = jnp.stack([taps, taps[::-1]])
    k1 = jnp.transpose(both, (0, 2, 1, 3)).reshape(2, HID, 9 * CPAD)
    x, e = exchange(state, mask, fold)
    return compute(x, e, k1, first_bias[None], second_kernel, second_bias[None])


def solution(mesh):
    return jax.shard_map(
        on_device,
        mesh=mesh,
        in_specs=(P(None, None, "lat", "lon"), P(None, "lat", "lon"), P("lon"), P(), P(), P(), P()),
        out_specs=P(None, None, "lat", "lon"),
        check_vma=False,
    )
```

```python
import functools

import jax
import jax.numpy as jnp
from jax import lax
from jax.experimental import pallas as pl
from jax.experimental.pallas import tpu as pltpu
from jax.sharding import PartitionSpec as P

F32 = jnp.float32
BF16 = jnp.bfloat16
MESH = pl.DeviceIdType.MESH
VMEM = pl.BlockSpec(memory_space=pltpu.VMEM)
SMEM = pl.BlockSpec(memory_space=pltpu.SMEM)

SAMPLES, CIN, ROWS, COLS, HID = 4, 75, 8, 256, 256
CPAD = 80
WIDE = SAMPLES * COLS
XROWS = ROWS + 4
HROWS = ROWS + 2
NLON, NLAT = 16, 8
LIMIT = 60 * 1024 * 1024


def lanes_of(shape):
    return lax.broadcasted_iota(jnp.int32, shape, len(shape) - 1)


def edge_pairs(x_ref, rows, pairs):
    pair = lax.shift_right_logical(lanes_of((CPAD, 128)), 1)
    pairs = list(pairs)
    for r in rows:
        for s in range(SAMPLES):
            row = x_ref[r, :, s * COLS : (s + 1) * COLS].astype(F32)
            at = 8 * r + 2 * s
            here = pair == at // 2
            for n, (half, by) in enumerate(((0, at), (0, at - 2), (1, at + 4), (1, at + 2))):
                part = pltpu.roll(row[:, half * 128 : half * 128 + 128], by % 128, 1)
                pairs[n] = jnp.where(here, part, pairs[n])
    return pairs


def prepare(state_ref, mask_ref, x_ref, t_ref):
    for s in range(SAMPLES):
        for h in range(2):
            cut = slice(h * 128, (h + 1) * 128)
            t_ref[s, h, CIN * ROWS : (CIN + 1) * ROWS, :] = mask_ref[0, :, cut].astype(F32)
            t_ref[s, h, (CIN + 1) * ROWS :, :] = jnp.zeros(((CPAD - CIN - 1) * ROWS, 128), F32)
            masked = state_ref[s, :, :, cut].astype(F32) * mask_ref[:, :, cut].astype(F32)
            t_ref[s, h, : CIN * ROWS, :] = masked.reshape(CIN * ROWS, 128)
            for r in range(ROWS):
                at = s * COLS + h * 128
                x_ref[r + 2, :, at : at + 128] = t_ref[s, h, pl.ds(r, CPAD, stride=ROWS), :].astype(BF16)


def piece(i):
    return i // 8, (i // 2) % 4, i % 2


HALF = ((0, 48), (48, 32))
EARLY = (2, 3, 4, 5)


def gelu(x):
    return 0.5 * x * (1.0 + jnp.tanh(0.7978845608028654 * (x + 0.044715 * (x * x * x))))


def wide_bias(ref):
    return jnp.transpose(jnp.broadcast_to(ref[...], (128, HID)))


def stack_taps(raw_ref, pad_ref, k1_ref, turned):
    lane = lanes_of((HID, 128))
    blocks = [None] * 6
    for t in range(9):
        if not turned:
            pad_ref[t, :, CIN:] = jnp.zeros((HID, 128 - CIN), F32)
            pad_ref[t, :, :CIN] = raw_ref[t].astype(F32)
        at = CPAD * (8 - t if turned else t)
        q, p = at // 128, at % 128
        moved = pltpu.roll(pad_ref[t], p, 1) if p else pad_ref[t]
        for block, keep in ((q, lane >= p), (q + 1, lane < p)):
            if block == q + 1 and p + CIN <= 128:
                continue
            part = jnp.where(keep, moved, 0.0)
            blocks[block] = part if blocks[block] is None else blocks[block] + part
    for n, block in enumerate(blocks):
        wide = min(128, 9 * CPAD - n * 128)
        k1_ref[1 if turned else 0, :, n * 128 : n * 128 + wide] = block[:, :wide].astype(BF16)


def shift_row(x_ref, xb_ref, r):
    row = x_ref[r].astype(F32)
    xb_ref[r, :CPAD, :] = pltpu.roll(row, 1, 1).astype(BF16)
    xb_ref[r, CPAD : 2 * CPAD, :] = x_ref[r]
    xb_ref[r, 2 * CPAD :, :] = pltpu.roll(row, WIDE - 1, 1).astype(BF16)


def hidden_row(x_ref, xb_ref, hb_ref, k1_ref, bias, which, r):
    kernel = k1_ref[which]
    taps = xb_ref[r : r + 3].reshape(9 * CPAD, WIDE)
    for pair in range(2):
        cut = slice(pair * 2 * COLS, (pair + 1) * 2 * COLS)
        out = jnp.dot(kernel, taps[:, cut], preferred_element_type=F32)
        surface = x_ref[r + 1, 64:CPAD, cut].astype(F32)[CIN - 64 : CIN - 63]
        out = gelu(out + jnp.concatenate([bias] * 4, 1)) * surface
        hb_ref[r, :HID, cut] = pltpu.roll(out, 1, 1).astype(BF16)
        hb_ref[r, HID : 2 * HID, cut] = out.astype(BF16)
        hb_ref[r, 2 * HID :, cut] = pltpu.roll(out, 2 * COLS - 1, 1).astype(BF16)


def output_row(x_ref, hb_ref, k2_ref, y_ref, bias, r):
    kernel = jnp.concatenate([k2_ref[t] for t in range(9)], 1)
    taps = hb_ref[r : r + 3].reshape(9 * HID, WIDE)
    for pair in range(2):
        cut = slice(pair * 2 * COLS, (pair + 1) * 2 * COLS)
        out = jnp.dot(kernel, taps[:, cut], preferred_element_type=F32)
        surface = x_ref[r + 2, 64:CPAD, cut].astype(F32)[CIN - 64 : CIN - 63]
        out = ((out + jnp.concatenate([bias] * 4, 1)) * surface).astype(BF16)
        y_ref[r, 2 * pair] = out[:, :COLS]
        y_ref[r, 2 * pair + 1] = out[:, COLS:]


def edge_columns(columns, k1_ref, k2_ref, bias1, bias2, top):
    lane = lanes_of((HID, 128))
    back = [[c if not a else pltpu.roll(c, 128 - 8 * a, 1) for a in range(3)] for c in columns]
    taps = jnp.concatenate(
        [jnp.concatenate([back[i + b][a] for a in range(3) for b in range(3)], 0).astype(BF16) for i in range(4)], 1
    )
    plain = jnp.dot(k1_ref[0], taps, preferred_element_type=F32)
    turned = jnp.dot(k1_ref[1], taps, preferred_element_type=F32)
    ghost = lane >= jnp.where(top, 72, 128)
    hidden = []
    for i in range(4):
        cut = slice(i * 128, (i + 1) * 128)
        out = jnp.where(ghost, turned[:, cut], plain[:, cut]) + bias1
        out = gelu(out) * back[i + 1][1][CIN : CIN + 1, :]
        hidden.append([out if not a else pltpu.roll(out, 128 - 8 * a, 1) for a in range(3)])
    taps = jnp.concatenate(
        [jnp.concatenate([hidden[i + b][a] for a in range(3) for b in range(3)], 0).astype(BF16) for i in range(2)], 1
    )
    kernel = jnp.concatenate([k2_ref[t] for t in range(9)], 1)
    out = jnp.dot(kernel, taps, preferred_element_type=F32)
    first, second = ((out[:, i * 128 : i * 128 + 128] + bias2) * back[i + 2][2][CIN : CIN + 1, :] for i in range(2))
    even = jnp.bitwise_and(lane, 1) == 0
    return jnp.where(even, first, pltpu.roll(second, 1, 1)), jnp.where(even, pltpu.roll(first, 127, 1), second)


def fold_kernel_parts(a_ref, y0_ref, y1_ref, s_ref, se_ref, fold_ref, lon):
    start = fold_ref[0]
    turn = jnp.bitwise_and(start, COLS - 1)
    block = lax.shift_right_logical(start, 8)
    source = lax.broadcasted_iota(jnp.int32, (COLS, COLS), 0)
    lane = lax.broadcasted_iota(jnp.int32, (COLS, COLS), 1)
    pieces = a_ref[...].reshape(NLON * 48, COLS)
    for y_ref, target in ((y0_ref, turn), (y1_ref, turn + COLS)):
        choose = jnp.where(source + lane == target, 1.0, 0.0).astype(BF16)
        y_ref[...] = jnp.dot(pieces, choose, preferred_element_type=F32).astype(BF16).reshape(NLON, 48, COLS)
    for d in range(NLON):
        b = jnp.bitwise_and(block + lon - d, NLON - 1)
        s_ref[d] = y0_ref[b] + y1_ref[jnp.bitwise_and(b + NLON - 1, NLON - 1)]
    group = lax.shift_right_logical(lane, 4)
    step = jnp.where(group >= 8, group - 16, group)
    k = jnp.bitwise_and(lane, 15)
    column = jnp.where(k < 2, k - 2, k + COLS - 2)
    hit = jnp.logical_and(k < 4, source == turn - column - COLS * step)
    outer = jnp.dot(pieces, jnp.where(hit, 1.0, 0.0).astype(BF16), preferred_element_type=F32).reshape(NLON, 48, COLS)
    total = jnp.zeros((48, COLS), F32)
    for e in range(NLON):
        total = total + pltpu.roll(outer[e], jnp.bitwise_and(16 * (block + lon - e), COLS - 1), 1)
    total = jnp.concatenate([total, jnp.zeros((80, COLS), F32)], 0)
    se_ref[...] = jnp.transpose(total).astype(BF16).reshape(NLON, 16, 128)


def fold_edges(fe_ref):
    sent = jnp.transpose(fe_ref[...].reshape(NLON * 16, 128).astype(F32)).astype(BF16)
    f = lax.broadcasted_iota(jnp.int32, (256, 512), 0)
    lane = lax.broadcasted_iota(jnp.int32, (256, 512), 1)
    to_lane, side, half = jnp.bitwise_and(lane, 127), jnp.bitwise_and(lane // 128, 1), lane // 256
    hit = jnp.logical_and(
        jnp.bitwise_and(f // 16, 1) == half,
        jnp.logical_and(
            jnp.bitwise_and(f, 15) == 2 * side + jnp.bitwise_and(to_lane, 1),
            to_lane // 2 == 40 + (f // 128) * 4 + jnp.bitwise_and(f // 32, 3),
        ),
    )
    got = jnp.dot(sent, jnp.where(hit, 1.0, 0.0).astype(BF16), preferred_element_type=F32)
    return [jnp.concatenate([got[:48, n : n + 128], got[:32, 256 + n : 384 + n]], 0) for n in (0, 128)]


def main_kernel(
    state_hbm, mask_hbm, fold_ref, k1_hbm, b1_ref, k2_hbm, b2_ref, y_hbm, edge_out,
    state_ref, mask_ref, k1_raw, k1_pad, k1_ref, k2_ref, x_ref, t_ref, xb_ref, hb_ref, y_ref,
    sp_ref, lp_ref, rp_ref, a_ref, y0_ref, y1_ref, s_ref, se_ref, fe_ref, ft_ref,
    load_sem, store_sem,
    row_send, row_recv, edge_send, edge_recv, f1_send, f1_recv, f2_send, f2_recv, f3_send, f3_recv,
):
    loads = [
        pltpu.make_async_copy(src, dst, load_sem.at[n])
        for n, (src, dst) in enumerate(((mask_hbm, mask_ref), (state_hbm, state_ref), (k1_hbm, k1_raw), (k2_hbm, k2_ref)))
    ]
    for load in loads:
        load.start()
    lon = lax.axis_index("lon")
    lat = lax.axis_index("lat")
    right, left = lax.rem(lon + 1, NLON), lax.rem(lon + NLON - 1, NLON)
    top = lat == NLAT - 1
    has = {-1: lat > 0, 0: None, 1: lat < NLAT - 1}

    def when(flag, fn):
        if flag is None:
            fn()
        else:
            pl.when(flag)(fn)

    barrier = pltpu.get_barrier_semaphore()

    def greet(at_lat, at_lon):
        pl.semaphore_signal(barrier, inc=1, device_id={"lat": at_lat, "lon": at_lon}, device_id_type=MESH)

    for d in (-1, 0, 1):
        def hello(d=d):
            if d:
                greet(lat + d, lon)
            greet(lat + d, left)
            greet(lat + d, right)
        when(has[d], hello)

    @pl.when(top)
    def _():
        for k in range(2, NLON - 1):
            greet(lat, lax.rem(lon + k, NLON))

    loads[0].wait()
    loads[1].wait()
    prepare(state_ref, mask_ref, x_ref, t_ref)
    pairs = edge_pairs(x_ref, range(2, 2 + ROWS), [jnp.zeros((CPAD, 128), F32)] * 4)
    sp_ref[0] = pairs[0].astype(BF16)
    sp_ref[1] = pairs[3].astype(BF16)
    loads[2].wait()
    stack_taps(k1_raw, k1_pad, k1_ref, False)
    bias1, bias2 = wide_bias(b1_ref), wide_bias(b2_ref)

    def hidden(r, which=0):
        hidden_row(x_ref, xb_ref, hb_ref, k1_ref, bias1, which, r)

    stores = []

    def output(r):
        output_row(x_ref, hb_ref, k2_ref, y_ref, bias2, r)
        stores.append(pltpu.make_async_copy(y_ref.at[r], y_hbm.at[:, r], store_sem.at[r]))
        stores[-1].start()

    for r in range(2, 2 + ROWS):
        shift_row(x_ref, xb_ref, r)
    for r in EARLY:
        hidden(r)

    @pl.when(lat == 0)
    def _():
        x_ref[0:2] = jnp.zeros((2, CPAD, WIDE), BF16)
        lp_ref[0] = jnp.zeros((CPAD, 128), BF16)
        rp_ref[0] = jnp.zeros((CPAD, 128), BF16)

    @pl.when(jnp.logical_and(lat > 0, lat < NLAT - 1))
    def _():
        pl.semaphore_wait(barrier, 8)

    @pl.when(lat == 0)
    def _():
        pl.semaphore_wait(barrier, 5)

    @pl.when(top)
    def _():
        pl.semaphore_wait(barrier, 18)

    def to(src, dst, send, recv, at_lat, at_lon):
        return pltpu.make_async_remote_copy(
            src_ref=src, dst_ref=dst, send_sem=send, recv_sem=recv,
            device_id={"lat": at_lat, "lon": at_lon}, device_id_type=MESH,
        )

    def first_copy(i):
        row, s, half = piece(i)
        at, n = HALF[half]
        return to(
            x_ref.at[9 - row, pl.ds(at, n), pl.ds(s * COLS, COLS)], a_ref.at[lon, pl.ds(0, n)],
            f1_send.at[i], f1_recv.at[lon], lat, i,
        )

    my_row, my_s, my_half = piece(lon)

    def second_copy(d, half):
        at, n = HALF[half]
        return to(
            s_ref.at[d, pl.ds(0, n)],
            x_ref.at[10 + my_row, pl.ds(at, n), pl.ds(pl.multiple_of(my_s * COLS, COLS), COLS)],
            f2_send.at[d], f2_recv.at[lon], lat, d,
        )

    def third_copy(d):
        return to(se_ref.at[d], fe_ref.at[lon], f3_send.at[d], f3_recv.at[lon], lat, d)

    up = to(x_ref.at[pl.ds(8, 2)], x_ref.at[pl.ds(0, 2)], row_send.at[0], row_recv.at[0], lat + 1, lon)
    down = to(x_ref.at[pl.ds(2, 2)], x_ref.at[pl.ds(10, 2)], row_send.at[1], row_recv.at[1], lat - 1, lon)
    edge = {}
    for d in (-1, 0, 1):
        edge[d] = (
            to(sp_ref.at[0], rp_ref.at[1 - d], edge_send.at[d + 1], edge_recv.at[1 - d], lat + d, left),
            to(sp_ref.at[1], lp_ref.at[1 - d], edge_send.at[d + 4], edge_recv.at[4 - d], lat + d, right),
        )

    @pl.when(top)
    def _():
        for i in range(NLON):
            pl.when(i != lon)(lambda i=i: first_copy(i).start())

    for d in (-1, 0, 1):
        def go(d=d):
            edge[d][0].start()
            edge[d][1].start()
        when(has[d], go)
    pl.when(has[1])(lambda: up.start())
    pl.when(has[-1])(lambda: down.start())

    for r in range(2, HROWS - 2):
        if r not in EARLY:
            hidden(r)
    loads[3].wait()
    for r in (2, 3, 4):
        output(r)

    @pl.when(top)
    def _():
        for half in (0, 1):
            at, n = HALF[half]

            @pl.when(my_half == half)
            def _():
                mine = x_ref.at[9 - my_row, pl.ds(at, n), pl.ds(pl.multiple_of(my_s * COLS, COLS), COLS)]
                a_ref[lon, 0:n] = mine[...]
                if n < 48:
                    a_ref[:, n:] = jnp.zeros((NLON, 48 - n, COLS), BF16)
                for e in range(NLON):
                    def arrive(e=e):
                        to(a_ref.at[e, pl.ds(0, n)], a_ref.at[e, pl.ds(0, n)], f1_send.at[e], f1_recv.at[e], lat, e).wait_recv()
                    pl.when(e != lon)(arrive)

        fold_kernel_parts(a_ref, y0_ref, y1_ref, s_ref, se_ref, fold_ref, lon)
        for half in (0, 1):
            at, n = HALF[half]

            @pl.when(my_half == half)
            def _():
                for d in range(NLON):
                    pl.when(d != lon)(lambda d=d: second_copy(d, half).start())
                x_ref[10 + my_row, at : at + n, pl.ds(pl.multiple_of(my_s * COLS, COLS), COLS)] = s_ref[lon, 0:n]
        for d in range(NLON):
            pl.when(d != lon)(lambda d=d: third_copy(d).start())
        fe_ref[lon] = se_ref[lon]

    output(5)

    @pl.when(top)
    def _():
        stack_taps(k1_raw, k1_pad, k1_ref, True)

    pl.when(has[-1])(lambda: up.wait_recv())
    shift_row(x_ref, xb_ref, 0)
    shift_row(x_ref, xb_ref, 1)
    hidden(1)
    hidden(0)
    output(1)
    output(0)

    for d in (-1, 0, 1):
        def got(d=d):
            edge[-d][0].wait_recv()
            edge[-d][1].wait_recv()
        when(has[d], got)
    pl.when(has[1])(lambda: down.wait_recv())

    @pl.when(top)
    def _():
        for e in range(NLON):
            row, s, half = piece(e)
            at, n = HALF[half]
            def arrive(e=e, row=row, s=s, at=at, n=n):
                there = x_ref.at[10 + row, pl.ds(at, n), pl.ds(s * COLS, COLS)]
                to(there, there, f2_send.at[e], f2_recv.at[e], lat, e).wait_recv()
                to(fe_ref.at[e], fe_ref.at[e], f3_send.at[e], f3_recv.at[e], lat, e).wait_recv()
            pl.when(e != lon)(arrive)
        for n, part in enumerate(fold_edges(fe_ref)):
            ft_ref[n] = part

    shift_row(x_ref, xb_ref, ROWS + 2)
    shift_row(x_ref, xb_ref, ROWS + 3)
    hidden(ROWS)
    hidden(ROWS + 1, jnp.where(top, 1, 0))
    output(6)
    output(7)

    pairs = edge_pairs(x_ref, (0, 1, 10, 11), pairs)
    lane = lanes_of((CPAD, 128))

    def joined(ref, n):
        below = pltpu.roll(ref[0].astype(F32), 64, 1)
        above = jnp.where(top, ft_ref[n], pltpu.roll(ref[2].astype(F32), 64, 1))
        return jnp.where(lane < 16, below, jnp.where(lane < 80, ref[1].astype(F32), above))

    before, after = joined(lp_ref, 0), joined(rp_ref, 1)
    even = jnp.bitwise_and(lane, 1) == 0
    columns = []
    for low, high in ((before, pairs[2]), (pairs[0], pairs[3]), (pairs[1], after)):
        columns.append(jnp.where(even, low, pltpu.roll(high, 1, 1)))
        columns.append(jnp.where(even, pltpu.roll(low, 127, 1), high))
    first, last = edge_columns(columns, k1_ref, k2_ref, bias1, bias2, top)
    edge_out[0] = first
    edge_out[1] = last

    pl.when(has[1])(lambda: up.wait_send())
    pl.when(has[-1])(lambda: down.wait_send())
    for d in (-1, 0, 1):
        def sent(d=d):
            edge[d][0].wait_send()
            edge[d][1].wait_send()
        when(has[d], sent)

    @pl.when(top)
    def _():
        for i in range(NLON):
            pl.when(i != lon)(lambda i=i: first_copy(i).wait_send())
        for half in (0, 1):
            @pl.when(my_half == half)
            def _():
                for d in range(NLON):
                    pl.when(d != lon)(lambda d=d: second_copy(d, half).wait_send())
        for d in range(NLON):
            pl.when(d != lon)(lambda d=d: third_copy(d).wait_send())
    for store in stores:
        store.wait()


HBM = pl.BlockSpec(memory_space=pl.ANY)


def main(state, mask, fold, k1, b1, k2, b2):
    dma = pltpu.SemaphoreType.DMA
    return pl.pallas_call(
        main_kernel,
        out_shape=(
            jax.ShapeDtypeStruct((SAMPLES, ROWS, HID, COLS), BF16),
            jax.ShapeDtypeStruct((2, HID, 128), F32),
        ),
        in_specs=[HBM, HBM, SMEM, HBM, VMEM, HBM, VMEM],
        out_specs=(HBM, VMEM),
        scratch_shapes=[
            pltpu.VMEM(state.shape, BF16),
            pltpu.VMEM(mask.shape, jnp.int32),
            pltpu.VMEM(k1.shape, BF16),
            pltpu.VMEM((9, HID, 128), F32),
            pltpu.VMEM((2, HID, 9 * CPAD), BF16),
            pltpu.VMEM(k2.shape, BF16),
            pltpu.VMEM((XROWS, CPAD, WIDE), BF16),
            pltpu.VMEM((SAMPLES, 2, CPAD * ROWS, 128), F32),
            pltpu.VMEM((XROWS, 3 * CPAD, WIDE), BF16),
            pltpu.VMEM((HROWS, 3 * HID, WIDE), BF16),
            pltpu.VMEM((ROWS, SAMPLES, HID, COLS), BF16),
            pltpu.VMEM((2, CPAD, 128), BF16),
            pltpu.VMEM((3, CPAD, 128), BF16),
            pltpu.VMEM((3, CPAD, 128), BF16),
            pltpu.VMEM((NLON, 48, COLS), BF16),
            pltpu.VMEM((NLON, 48, COLS), BF16),
            pltpu.VMEM((NLON, 48, COLS), BF16),
            pltpu.VMEM((NLON, 48, COLS), BF16),
            pltpu.VMEM((NLON, 16, 128), BF16),
            pltpu.VMEM((NLON, 16, 128), BF16),
            pltpu.VMEM((2, CPAD, 128), F32),
            dma((4,)), dma((ROWS,)),
            dma((2,)), dma((2,)), dma((6,)), dma((6,)),
            dma((NLON,)), dma((NLON,)), dma((NLON,)), dma((NLON,)), dma((NLON,)), dma((NLON,)),
        ],
        compiler_params=pltpu.CompilerParams(collective_id=0, has_side_effects=True, vmem_limit_bytes=LIMIT),
    )(state, mask, fold, k1, b1, k2, b2)


CHANNELS = 128


def order_kernel(y_ref, edge_ref, out_ref, t_ref):
    s = pl.program_id(0)
    lane = lanes_of((CHANNELS, 128))
    first = pltpu.roll(edge_ref[0], lax.rem(128 - 2 * s, 128), 1)
    last = pltpu.roll(edge_ref[1], lax.rem(126 - 2 * s, 128), 1)
    for r in range(ROWS):
        by = (128 - 8 * r) % 128
        low, high = (pltpu.roll(v, by, 1) if r else v for v in (first, last))
        t_ref[0, pl.ds(r, CHANNELS, stride=ROWS), :] = jnp.where(lane < 2, low, y_ref[0, r, :, :128].astype(F32))
        t_ref[1, pl.ds(r, CHANNELS, stride=ROWS), :] = jnp.where(lane >= 126, high, y_ref[0, r, :, 128:].astype(F32))
    for h in range(2):
        out_ref[0, :, :, h * 128 : (h + 1) * 128] = t_ref[h].reshape(CHANNELS, ROWS, 128).astype(BF16)


def order(y, edges):
    return pl.pallas_call(
        order_kernel,
        grid=(SAMPLES, HID // CHANNELS),
        out_shape=jax.ShapeDtypeStruct((SAMPLES, HID, ROWS, COLS), BF16),
        in_specs=[
            pl.BlockSpec((1, ROWS, CHANNELS, COLS), lambda s, c: (s, 0, c, 0)),
            pl.BlockSpec((2, CHANNELS, 128), lambda s, c: (0, c, 0)),
        ],
        out_specs=pl.BlockSpec((1, CHANNELS, ROWS, COLS), lambda s, c: (s, c, 0, 0)),
        scratch_shapes=[pltpu.VMEM((2, CHANNELS * ROWS, 128), F32)],
        compiler_params=pltpu.CompilerParams(vmem_limit_bytes=LIMIT),
    )(y, edges)


def on_device(state, mask, fold, first_kernel, first_bias, second_kernel, second_bias):
    y, edges = main(state, mask, fold, first_kernel, first_bias[None], second_kernel, second_bias[None])
    return order(y, edges)


def solution(mesh):
    return jax.shard_map(
        on_device,
        mesh=mesh,
        in_specs=(P(None, None, "lat", "lon"), P(None, "lat", "lon"), P("lon"), P(), P(), P(), P()),
        out_specs=P(None, None, "lat", "lon"),
        check_vma=False,
    )
```

```python
import functools

import jax
import jax.numpy as jnp
from jax import lax
from jax.experimental import pallas as pl
from jax.experimental.pallas import tpu as pltpu
from jax.sharding import PartitionSpec as P

F32 = jnp.float32
BF16 = jnp.bfloat16
MESH = pl.DeviceIdType.MESH
VMEM = pl.BlockSpec(memory_space=pltpu.VMEM)
SMEM = pl.BlockSpec(memory_space=pltpu.SMEM)

SAMPLES, CIN, ROWS, COLS, HID = 4, 75, 8, 256, 256
CPAD = 80
WIDE = SAMPLES * COLS
XROWS = ROWS + 4
HROWS = ROWS + 2
NLON, NLAT = 16, 8
LIMIT = 60 * 1024 * 1024


def lanes_of(shape):
    return lax.broadcasted_iota(jnp.int32, shape, len(shape) - 1)


def edge_pairs(x_ref, rows, pairs):
    pair = lax.shift_right_logical(lanes_of((CPAD, 128)), 1)
    pairs = list(pairs)
    for r in rows:
        for s in range(SAMPLES):
            row = x_ref[r, :, s * COLS : (s + 1) * COLS].astype(F32)
            at = 8 * r + 2 * s
            here = pair == at // 2
            for n, (half, by) in enumerate(((0, at), (0, at - 2), (1, at + 4), (1, at + 2))):
                part = pltpu.roll(row[:, half * 128 : half * 128 + 128], by % 128, 1)
                pairs[n] = jnp.where(here, part, pairs[n])
    return pairs


def prepare(state_ref, mask_ref, x_ref, t_ref):
    for s in range(SAMPLES):
        for h in range(2):
            cut = slice(h * 128, (h + 1) * 128)
            t_ref[s, h, CIN * ROWS : (CIN + 1) * ROWS, :] = mask_ref[0, :, cut].astype(F32)
            t_ref[s, h, (CIN + 1) * ROWS : (CIN + 4) * ROWS, :] = jnp.ones((3 * ROWS, 128), F32)
            t_ref[s, h, (CIN + 4) * ROWS :, :] = jnp.zeros(((CPAD - CIN - 4) * ROWS, 128), F32)
            masked = state_ref[s, :, :, cut].astype(F32) * mask_ref[:, :, cut].astype(F32)
            t_ref[s, h, : CIN * ROWS, :] = masked.reshape(CIN * ROWS, 128)
            for r in range(ROWS):
                at = s * COLS + h * 128
                x_ref[r + 2, :, at : at + 128] = t_ref[s, h, pl.ds(r, CPAD, stride=ROWS), :].astype(BF16)


def piece(i):
    return i // 8, (i // 2) % 4, i % 2


HALF = ((0, 48), (48, 32))
EARLY = (2, 3, 4, 5)


def gelu_times(x, half_surface):
    half = x * half_surface
    return half + half * jnp.tanh(x * (0.7978845608028654 + 0.035677408136300125 * (x * x)))


def wide_bias(ref):
    return jnp.transpose(jnp.broadcast_to(ref[...], (128, HID)))


def stack_taps(raw_ref, bias_ref, pad_ref, k1_ref, turned):
    pad_ref[9 * CPAD :, :] = jnp.zeros((pad_ref.shape[0] - 9 * CPAD, HID), F32)
    for t in range(9):
        at = CPAD * (8 - t if turned else t)
        pad_ref[at + 72 : at + CPAD, :] = jnp.zeros((8, HID), F32)
        pad_ref[at : at + CIN, :] = raw_ref[t].astype(F32)
    at = 4 * CPAD + CIN + 1
    rest = bias_ref[...]
    for n in range(3):
        part = rest.astype(BF16).astype(F32)
        pad_ref[at + n : at + n + 1, :] = part
        rest = rest - part
    k1_ref[1 if turned else 0] = jnp.transpose(pad_ref[...])[:, : 9 * CPAD].astype(BF16)


def shift_row(x_ref, xb_ref, r):
    row = x_ref[r]
    xb_ref[r, :CPAD, :] = pltpu.roll(row, 1, 1)
    xb_ref[r, CPAD : 2 * CPAD, :] = row
    xb_ref[r, 2 * CPAD :, :] = pltpu.roll(row, WIDE - 1, 1)


def hidden_row(x_ref, xb_ref, hb_ref, k1_ref, which, r):
    kernel = k1_ref[which]
    taps = xb_ref[r : r + 3].reshape(9 * CPAD, WIDE)
    for pair in range(2):
        cut = slice(pair * 2 * COLS, (pair + 1) * 2 * COLS)
        out = jnp.dot(kernel, taps[:, cut], preferred_element_type=F32)
        surface = x_ref[r + 1, 64:CPAD, cut].astype(F32)[CIN - 64 : CIN - 63]
        out = gelu_times(out, 0.5 * surface).astype(BF16)
        hb_ref[r, :HID, cut] = pltpu.roll(out, 1, 1)
        hb_ref[r, HID : 2 * HID, cut] = out
        hb_ref[r, 2 * HID :, cut] = pltpu.roll(out, 2 * COLS - 1, 1)


def output_row(x_ref, hb_ref, k2_ref, y_ref, bias, r):
    kernel = jnp.concatenate([k2_ref[t] for t in range(9)], 1)
    taps = hb_ref[r : r + 3].reshape(9 * HID, WIDE)
    column = jnp.bitwise_and(lanes_of((1, 2 * COLS)), COLS - 1)
    inner = jnp.logical_and(column >= 2, column < COLS - 2)
    for pair in range(2):
        cut = slice(pair * 2 * COLS, (pair + 1) * 2 * COLS)
        out = jnp.dot(kernel, taps[:, cut], preferred_element_type=F32)
        surface = x_ref[r + 2, 64:CPAD, cut].astype(F32)[CIN - 64 : CIN - 63]
        surface = jnp.where(inner, surface, 0.0)
        out = ((out + jnp.concatenate([bias] * 4, 1)) * surface).astype(BF16)
        y_ref[r, 2 * pair] = out[:, :COLS]
        y_ref[r, 2 * pair + 1] = out[:, COLS:]


def edge_columns(columns, k1_ref, k2_ref, bias2, top):
    lane = lanes_of((HID, 128))
    back = [[c if not a else pltpu.roll(c, 128 - 8 * a, 1) for a in range(3)] for c in columns]
    taps = jnp.concatenate(
        [jnp.concatenate([back[i + b][a] for a in range(3) for b in range(3)], 0).astype(BF16) for i in range(4)], 1
    )
    plain = jnp.dot(k1_ref[0], taps, preferred_element_type=F32)
    turned = jnp.dot(k1_ref[1], taps, preferred_element_type=F32)
    ghost = lane >= jnp.where(top, 72, 128)
    hidden = []
    for i in range(4):
        cut = slice(i * 128, (i + 1) * 128)
        out = jnp.where(ghost, turned[:, cut], plain[:, cut])
        out = gelu_times(out, 0.5 * back[i + 1][1][CIN : CIN + 1, :])
        hidden.append([out if not a else pltpu.roll(out, 128 - 8 * a, 1) for a in range(3)])
    taps = jnp.concatenate(
        [jnp.concatenate([hidden[i + b][a] for a in range(3) for b in range(3)], 0).astype(BF16) for i in range(2)], 1
    )
    kernel = jnp.concatenate([k2_ref[t] for t in range(9)], 1)
    out = jnp.dot(kernel, taps, preferred_element_type=F32)
    first, second = ((out[:, i * 128 : i * 128 + 128] + bias2) * back[i + 2][2][CIN : CIN + 1, :] for i in range(2))
    even = jnp.bitwise_and(lane, 1) == 0
    return jnp.where(even, first, pltpu.roll(second, 1, 1)), jnp.where(even, pltpu.roll(first, 127, 1), second)


def fold_kernel_parts(a_ref, y0_ref, y1_ref, s_ref, se_ref, fold_ref, lon):
    start = fold_ref[0]
    turn = jnp.bitwise_and(start, COLS - 1)
    block = lax.shift_right_logical(start, 8)
    source = lax.broadcasted_iota(jnp.int32, (COLS, COLS), 0)
    lane = lax.broadcasted_iota(jnp.int32, (COLS, COLS), 1)
    pieces = a_ref[...].reshape(NLON * 48, COLS)
    for y_ref, target in ((y0_ref, turn), (y1_ref, turn + COLS)):
        choose = jnp.where(source + lane == target, 1.0, 0.0).astype(BF16)
        y_ref[...] = jnp.dot(pieces, choose, preferred_element_type=F32).astype(BF16).reshape(NLON, 48, COLS)
    for d in range(NLON):
        b = jnp.bitwise_and(block + lon - d, NLON - 1)
        s_ref[d] = y0_ref[b] + y1_ref[jnp.bitwise_and(b + NLON - 1, NLON - 1)]
    group = lax.shift_right_logical(lane, 4)
    step = jnp.where(group >= 8, group - 16, group)
    k = jnp.bitwise_and(lane, 15)
    column = jnp.where(k < 2, k - 2, k + COLS - 2)
    hit = jnp.logical_and(k < 4, source == turn - column - COLS * step)
    outer = jnp.dot(pieces, jnp.where(hit, 1.0, 0.0).astype(BF16), preferred_element_type=F32).reshape(NLON, 48, COLS)
    total = jnp.zeros((48, COLS), F32)
    for e in range(NLON):
        total = total + pltpu.roll(outer[e], jnp.bitwise_and(16 * (block + lon - e), COLS - 1), 1)
    total = jnp.concatenate([total, jnp.zeros((80, COLS), F32)], 0)
    se_ref[...] = jnp.transpose(total).astype(BF16).reshape(NLON, 16, 128)


def fold_edges(fe_ref):
    sent = jnp.transpose(fe_ref[...].reshape(NLON * 16, 128).astype(F32)).astype(BF16)
    f = lax.broadcasted_iota(jnp.int32, (256, 512), 0)
    lane = lax.broadcasted_iota(jnp.int32, (256, 512), 1)
    to_lane, side, half = jnp.bitwise_and(lane, 127), jnp.bitwise_and(lane // 128, 1), lane // 256
    hit = jnp.logical_and(
        jnp.bitwise_and(f // 16, 1) == half,
        jnp.logical_and(
            jnp.bitwise_and(f, 15) == 2 * side + jnp.bitwise_and(to_lane, 1),
            to_lane // 2 == 40 + (f // 128) * 4 + jnp.bitwise_and(f // 32, 3),
        ),
    )
    got = jnp.dot(sent, jnp.where(hit, 1.0, 0.0).astype(BF16), preferred_element_type=F32)
    return [jnp.concatenate([got[:48, n : n + 128], got[:32, 256 + n : 384 + n]], 0) for n in (0, 128)]


def main_kernel(
    state_hbm, mask_hbm, fold_ref, k1_hbm, b1_ref, k2_hbm, b2_ref, y_hbm, edge_out,
    state_ref, mask_ref, k1_raw, k1_pad, k1_ref, k2_ref, x_ref, t_ref, xb_ref, hb_ref, y_ref,
    sp_ref, lp_ref, rp_ref, a_ref, y0_ref, y1_ref, s_ref, se_ref, fe_ref, ft_ref,
    load_sem, store_sem,
    row_send, row_recv, edge_send, edge_recv, f1_send, f1_recv, f2_send, f2_recv, f3_send, f3_recv,
):
    loads = [
        pltpu.make_async_copy(src, dst, load_sem.at[n])
        for n, (src, dst) in enumerate(((mask_hbm, mask_ref), (state_hbm, state_ref), (k1_hbm, k1_raw), (k2_hbm, k2_ref)))
    ]
    for load in loads:
        load.start()
    lon = lax.axis_index("lon")
    lat = lax.axis_index("lat")
    right, left = lax.rem(lon + 1, NLON), lax.rem(lon + NLON - 1, NLON)
    top = lat == NLAT - 1
    has = {-1: lat > 0, 0: None, 1: lat < NLAT - 1}

    def when(flag, fn):
        if flag is None:
            fn()
        else:
            pl.when(flag)(fn)

    barrier = pltpu.get_barrier_semaphore()

    def greet(at_lat, at_lon):
        pl.semaphore_signal(barrier, inc=1, device_id={"lat": at_lat, "lon": at_lon}, device_id_type=MESH)

    for d in (-1, 0, 1):
        def hello(d=d):
            if d:
                greet(lat + d, lon)
            greet(lat + d, left)
            greet(lat + d, right)
        when(has[d], hello)

    @pl.when(top)
    def _():
        for k in range(2, NLON - 1):
            greet(lat, lax.rem(lon + k, NLON))

    loads[0].wait()
    loads[1].wait()
    prepare(state_ref, mask_ref, x_ref, t_ref)
    pairs = edge_pairs(x_ref, range(2, 2 + ROWS), [jnp.zeros((CPAD, 128), F32)] * 4)
    sp_ref[0] = pairs[0].astype(BF16)
    sp_ref[1] = pairs[3].astype(BF16)
    loads[2].wait()
    stack_taps(k1_raw, b1_ref, k1_pad, k1_ref, False)
    bias2 = wide_bias(b2_ref)

    def hidden(r, which=0):
        hidden_row(x_ref, xb_ref, hb_ref, k1_ref, which, r)

    stores = []

    def output(r):
        output_row(x_ref, hb_ref, k2_ref, y_ref, bias2, r)
        stores.append(pltpu.make_async_copy(y_ref.at[r], y_hbm.at[:, r], store_sem.at[r]))
        stores[-1].start()

    for r in range(2, 2 + ROWS):
        shift_row(x_ref, xb_ref, r)
    for r in EARLY:
        hidden(r)

    @pl.when(lat == 0)
    def _():
        x_ref[0:2] = jnp.zeros((2, CPAD, WIDE), BF16)
        lp_ref[0] = jnp.zeros((CPAD, 128), BF16)
        rp_ref[0] = jnp.zeros((CPAD, 128), BF16)

    @pl.when(jnp.logical_and(lat > 0, lat < NLAT - 1))
    def _():
        pl.semaphore_wait(barrier, 8)

    @pl.when(lat == 0)
    def _():
        pl.semaphore_wait(barrier, 5)

    @pl.when(top)
    def _():
        pl.semaphore_wait(barrier, 18)

    def to(src, dst, send, recv, at_lat, at_lon):
        return pltpu.make_async_remote_copy(
            src_ref=src, dst_ref=dst, send_sem=send, recv_sem=recv,
            device_id={"lat": at_lat, "lon": at_lon}, device_id_type=MESH,
        )

    def first_copy(i):
        row, s, half = piece(i)
        at, n = HALF[half]
        return to(
            x_ref.at[9 - row, pl.ds(at, n), pl.ds(s * COLS, COLS)], a_ref.at[lon, pl.ds(0, n)],
            f1_send.at[i], f1_recv.at[lon], lat, i,
        )

    my_row, my_s, my_half = piece(lon)

    def second_copy(d, half):
        at, n = HALF[half]
        return to(
            s_ref.at[d, pl.ds(0, n)],
            x_ref.at[10 + my_row, pl.ds(at, n), pl.ds(pl.multiple_of(my_s * COLS, COLS), COLS)],
            f2_send.at[d], f2_recv.at[lon], lat, d,
        )

    def third_copy(d):
        return to(se_ref.at[d], fe_ref.at[lon], f3_send.at[d], f3_recv.at[lon], lat, d)

    up = to(x_ref.at[pl.ds(8, 2)], x_ref.at[pl.ds(0, 2)], row_send.at[0], row_recv.at[0], lat + 1, lon)
    down = to(x_ref.at[pl.ds(2, 2)], x_ref.at[pl.ds(10, 2)], row_send.at[1], row_recv.at[1], lat - 1, lon)
    edge = {}
    for d in (-1, 0, 1):
        edge[d] = (
            to(sp_ref.at[0], rp_ref.at[1 - d], edge_send.at[d + 1], edge_recv.at[1 - d], lat + d, left),
            to(sp_ref.at[1], lp_ref.at[1 - d], edge_send.at[d + 4], edge_recv.at[4 - d], lat + d, right),
        )

    @pl.when(top)
    def _():
        for i in range(NLON):
            pl.when(i != lon)(lambda i=i: first_copy(i).start())

    pl.when(has[1])(lambda: up.start())
    pl.when(has[-1])(lambda: down.start())

    for r in range(2, HROWS - 2):
        if r not in EARLY:
            hidden(r)
    loads[3].wait()
    for r in (2, 3, 4):
        output(r)

    @pl.when(top)
    def _():
        for half in (0, 1):
            at, n = HALF[half]

            @pl.when(my_half == half)
            def _():
                mine = x_ref.at[9 - my_row, pl.ds(at, n), pl.ds(pl.multiple_of(my_s * COLS, COLS), COLS)]
                a_ref[lon, 0:n] = mine[...]
                if n < 48:
                    a_ref[:, n:] = jnp.zeros((NLON, 48 - n, COLS), BF16)
                for e in range(NLON):
                    def arrive(e=e):
                        to(a_ref.at[e, pl.ds(0, n)], a_ref.at[e, pl.ds(0, n)], f1_send.at[e], f1_recv.at[e], lat, e).wait_recv()
                    pl.when(e != lon)(arrive)

        fold_kernel_parts(a_ref, y0_ref, y1_ref, s_ref, se_ref, fold_ref, lon)
        for half in (0, 1):
            at, n = HALF[half]

            @pl.when(my_half == half)
            def _():
                for d in range(NLON):
                    pl.when(d != lon)(lambda d=d: second_copy(d, half).start())
                x_ref[10 + my_row, at : at + n, pl.ds(pl.multiple_of(my_s * COLS, COLS), COLS)] = s_ref[lon, 0:n]
        for d in range(NLON):
            pl.when(d != lon)(lambda d=d: third_copy(d).start())
        fe_ref[lon] = se_ref[lon]

    for d in (-1, 0, 1):
        def go(d=d):
            edge[d][0].start()
            edge[d][1].start()
        when(has[d], go)

    output(5)

    @pl.when(top)
    def _():
        stack_taps(k1_raw, b1_ref, k1_pad, k1_ref, True)

    pl.when(has[-1])(lambda: up.wait_recv())
    shift_row(x_ref, xb_ref, 0)
    shift_row(x_ref, xb_ref, 1)
    hidden(1)
    hidden(0)
    output(1)
    output(0)

    for d in (-1, 0, 1):
        def got(d=d):
            edge[-d][0].wait_recv()
            edge[-d][1].wait_recv()
        when(has[d], got)
    pl.when(has[1])(lambda: down.wait_recv())

    @pl.when(top)
    def _():
        for e in range(NLON):
            row, s, half = piece(e)
            at, n = HALF[half]
            def arrive(e=e, row=row, s=s, at=at, n=n):
                there = x_ref.at[10 + row, pl.ds(at, n), pl.ds(s * COLS, COLS)]
                to(there, there, f2_send.at[e], f2_recv.at[e], lat, e).wait_recv()
                to(fe_ref.at[e], fe_ref.at[e], f3_send.at[e], f3_recv.at[e], lat, e).wait_recv()
            pl.when(e != lon)(arrive)
        for n, part in enumerate(fold_edges(fe_ref)):
            ft_ref[n] = part

    shift_row(x_ref, xb_ref, ROWS + 2)
    shift_row(x_ref, xb_ref, ROWS + 3)
    hidden(ROWS)
    hidden(ROWS + 1, jnp.where(top, 1, 0))
    output(6)
    output(7)

    pairs = edge_pairs(x_ref, (0, 1, 10, 11), pairs)
    lane = lanes_of((CPAD, 128))

    def joined(ref, n):
        below = pltpu.roll(ref[0].astype(F32), 64, 1)
        above = jnp.where(top, ft_ref[n], pltpu.roll(ref[2].astype(F32), 64, 1))
        return jnp.where(lane < 16, below, jnp.where(lane < 80, ref[1].astype(F32), above))

    before, after = joined(lp_ref, 0), joined(rp_ref, 1)
    even = jnp.bitwise_and(lane, 1) == 0
    columns = []
    for low, high in ((before, pairs[2]), (pairs[0], pairs[3]), (pairs[1], after)):
        columns.append(jnp.where(even, low, pltpu.roll(high, 1, 1)))
        columns.append(jnp.where(even, pltpu.roll(low, 127, 1), high))
    first, last = edge_columns(columns, k1_ref, k2_ref, bias2, top)
    edge_out[0] = first
    edge_out[1] = last

    pl.when(has[1])(lambda: up.wait_send())
    pl.when(has[-1])(lambda: down.wait_send())
    for d in (-1, 0, 1):
        def sent(d=d):
            edge[d][0].wait_send()
            edge[d][1].wait_send()
        when(has[d], sent)

    @pl.when(top)
    def _():
        for i in range(NLON):
            pl.when(i != lon)(lambda i=i: first_copy(i).wait_send())
        for half in (0, 1):
            @pl.when(my_half == half)
            def _():
                for d in range(NLON):
                    pl.when(d != lon)(lambda d=d: second_copy(d, half).wait_send())
        for d in range(NLON):
            pl.when(d != lon)(lambda d=d: third_copy(d).wait_send())
    for store in stores:
        store.wait()


HBM = pl.BlockSpec(memory_space=pl.ANY)


def main(state, mask, fold, k1, b1, k2, b2):
    dma = pltpu.SemaphoreType.DMA
    return pl.pallas_call(
        main_kernel,
        out_shape=(
            jax.ShapeDtypeStruct((SAMPLES, ROWS, HID, COLS), BF16),
            jax.ShapeDtypeStruct((2, HID, 128), F32),
        ),
        in_specs=[HBM, HBM, SMEM, HBM, VMEM, HBM, VMEM],
        out_specs=(HBM, VMEM),
        scratch_shapes=[
            pltpu.VMEM(state.shape, BF16),
            pltpu.VMEM(mask.shape, jnp.int32),
            pltpu.VMEM(k1.shape, BF16),
            pltpu.VMEM((6 * 128, HID), F32),
            pltpu.VMEM((2, HID, 9 * CPAD), BF16),
            pltpu.VMEM(k2.shape, BF16),
            pltpu.VMEM((XROWS, CPAD, WIDE), BF16),
            pltpu.VMEM((SAMPLES, 2, CPAD * ROWS, 128), F32),
            pltpu.VMEM((XROWS, 3 * CPAD, WIDE), BF16),
            pltpu.VMEM((HROWS, 3 * HID, WIDE), BF16),
            pltpu.VMEM((ROWS, SAMPLES, HID, COLS), BF16),
            pltpu.VMEM((2, CPAD, 128), BF16),
            pltpu.VMEM((3, CPAD, 128), BF16),
            pltpu.VMEM((3, CPAD, 128), BF16),
            pltpu.VMEM((NLON, 48, COLS), BF16),
            pltpu.VMEM((NLON, 48, COLS), BF16),
            pltpu.VMEM((NLON, 48, COLS), BF16),
            pltpu.VMEM((NLON, 48, COLS), BF16),
            pltpu.VMEM((NLON, 16, 128), BF16),
            pltpu.VMEM((NLON, 16, 128), BF16),
            pltpu.VMEM((2, CPAD, 128), F32),
            dma((4,)), dma((ROWS,)),
            dma((2,)), dma((2,)), dma((6,)), dma((6,)),
            dma((NLON,)), dma((NLON,)), dma((NLON,)), dma((NLON,)), dma((NLON,)), dma((NLON,)),
        ],
        compiler_params=pltpu.CompilerParams(collective_id=0, has_side_effects=True, vmem_limit_bytes=LIMIT),
    )(state, mask, fold, k1, b1, k2, b2)


CHANNELS = 128
CHUNKS = [(s, c) for s in range(SAMPLES) for c in range(HID // CHANNELS)]


def order_kernel(y_hbm, edge_ref, out_hbm, y_ref, out_ref, load_sem, store_sem):
    loads, stores = [], []
    for n, (s, c) in enumerate(CHUNKS):
        part = pl.ds(c * CHANNELS, CHANNELS)
        loads.append(pltpu.make_async_copy(y_hbm.at[s, :, part], y_ref.at[n], load_sem.at[n]))
        stores.append(pltpu.make_async_copy(out_ref.at[n], out_hbm.at[s, part], store_sem.at[n]))
    for load in loads:
        load.start()
    lane = lanes_of((CHANNELS, 128))
    for n, (s, c) in enumerate(CHUNKS):
        cut = slice(c * CHANNELS, (c + 1) * CHANNELS)
        first, last = edge_ref[0, cut], edge_ref[1, cut]
        loads[n].wait()
        for r in range(ROWS):
            at = 8 * r + 2 * s
            low = jnp.where(lane < 2, pltpu.roll(first, (128 - at) % 128, 1), 0.0)
            high = jnp.where(lane >= 126, pltpu.roll(last, (126 - at) % 128, 1), 0.0)
            y_ref[n, r, :, :128] = y_ref[n, r, :, :128] + low.astype(BF16)
            y_ref[n, r, :, 128:] = y_ref[n, r, :, 128:] + high.astype(BF16)
        out_ref[n] = jnp.swapaxes(y_ref[n], 0, 1)
        stores[n].start()
    for store in stores:
        store.wait()


def order(y, edges):
    return pl.pallas_call(
        order_kernel,
        out_shape=jax.ShapeDtypeStruct((SAMPLES, HID, ROWS, COLS), BF16),
        in_specs=[HBM, VMEM],
        out_specs=HBM,
        scratch_shapes=[
            pltpu.VMEM((len(CHUNKS), ROWS, CHANNELS, COLS), BF16),
            pltpu.VMEM((len(CHUNKS), CHANNELS, ROWS, COLS), BF16),
            pltpu.SemaphoreType.DMA((len(CHUNKS),)),
            pltpu.SemaphoreType.DMA((len(CHUNKS),)),
        ],
        compiler_params=pltpu.CompilerParams(vmem_limit_bytes=LIMIT),
    )(y, edges)


def on_device(state, mask, fold, first_kernel, first_bias, second_kernel, second_bias):
    y, edges = main(state, mask, fold, jnp.transpose(first_kernel, (0, 2, 1)), first_bias[None], second_kernel, second_bias[None])
    return order(y, edges)


def solution(mesh):
    return jax.shard_map(
        on_device,
        mesh=mesh,
        in_specs=(P(None, None, "lat", "lon"), P(None, "lat", "lon"), P("lon"), P(), P(), P(), P()),
        out_specs=P(None, None, "lat", "lon"),
        check_vma=False,
    )
```

```python
import functools

import jax
import jax.numpy as jnp
from jax import lax
from jax.experimental import pallas as pl
from jax.experimental.pallas import tpu as pltpu
from jax.sharding import PartitionSpec as P

F32 = jnp.float32
BF16 = jnp.bfloat16
MESH = pl.DeviceIdType.MESH
VMEM = pl.BlockSpec(memory_space=pltpu.VMEM)
SMEM = pl.BlockSpec(memory_space=pltpu.SMEM)

SAMPLES, CIN, ROWS, COLS, HID = 4, 75, 8, 256, 256
CPAD = 80
WIDE = SAMPLES * COLS
XROWS = ROWS + 4
HROWS = ROWS + 2
NLON, NLAT = 16, 8
LIMIT = 60 * 1024 * 1024


def lanes_of(shape):
    return lax.broadcasted_iota(jnp.int32, shape, len(shape) - 1)


def edge_pairs(x_ref, rows, pairs):
    pair = lax.shift_right_logical(lanes_of((CPAD, 128)), 1)
    pairs = list(pairs)
    for r in rows:
        for s in range(SAMPLES):
            row = x_ref[r, :, s * COLS : (s + 1) * COLS].astype(F32)
            at = 8 * r + 2 * s
            here = pair == at // 2
            for n, (half, by) in enumerate(((0, at), (0, at - 2), (1, at + 4), (1, at + 2))):
                part = pltpu.roll(row[:, half * 128 : half * 128 + 128], by % 128, 1)
                pairs[n] = jnp.where(here, part, pairs[n])
    return pairs


def prepare(state_ref, mask_ref, x_ref, t_ref):
    for s in range(SAMPLES):
        for h in range(2):
            cut = slice(h * 128, (h + 1) * 128)
            t_ref[s, h, CIN * ROWS : (CIN + 1) * ROWS, :] = mask_ref[0, :, cut].astype(F32)
            t_ref[s, h, (CIN + 1) * ROWS : (CIN + 4) * ROWS, :] = jnp.ones((3 * ROWS, 128), F32)
            t_ref[s, h, (CIN + 4) * ROWS :, :] = jnp.zeros(((CPAD - CIN - 4) * ROWS, 128), F32)
            masked = state_ref[s, :, :, cut].astype(F32) * mask_ref[:, :, cut].astype(F32)
            t_ref[s, h, : CIN * ROWS, :] = masked.reshape(CIN * ROWS, 128)
            for r in range(ROWS):
                at = s * COLS + h * 128
                x_ref[r + 2, :, at : at + 128] = t_ref[s, h, pl.ds(r, CPAD, stride=ROWS), :].astype(BF16)


def piece(i):
    return i // 8, (i // 2) % 4, i % 2


HALF = ((0, 48), (48, 32))
EARLY = (2, 3, 4, 5)


def gelu_times(x, half_surface):
    half = x * half_surface
    return half + half * jnp.tanh(x * (0.7978845608028654 + 0.035677408136300125 * (x * x)))


def wide_bias(ref):
    return jnp.transpose(jnp.broadcast_to(ref[...], (128, HID)))


def stack_taps(raw_ref, bias_ref, pad_ref, k1_ref, turned):
    pad_ref[9 * CPAD :, :] = jnp.zeros((pad_ref.shape[0] - 9 * CPAD, HID), F32)
    for t in range(9):
        at = CPAD * (8 - t if turned else t)
        pad_ref[at + 72 : at + CPAD, :] = jnp.zeros((8, HID), F32)
        pad_ref[at : at + CIN, :] = raw_ref[t].astype(F32)
    at = 4 * CPAD + CIN + 1
    rest = bias_ref[...]
    for n in range(3):
        part = rest.astype(BF16).astype(F32)
        pad_ref[at + n : at + n + 1, :] = part
        rest = rest - part
    k1_ref[1 if turned else 0] = jnp.transpose(pad_ref[...])[:, : 9 * CPAD].astype(BF16)


def shift_row(x_ref, xb_ref, r):
    row = x_ref[r]
    xb_ref[r, :CPAD, :] = pltpu.roll(row, 1, 1)
    xb_ref[r, CPAD : 2 * CPAD, :] = row
    xb_ref[r, 2 * CPAD :, :] = pltpu.roll(row, WIDE - 1, 1)


def hidden_row(x_ref, xb_ref, hb_ref, k1_ref, which, r):
    kernel = k1_ref[which]
    taps = xb_ref[r : r + 3].reshape(9 * CPAD, WIDE)
    for pair in range(2):
        cut = slice(pair * 2 * COLS, (pair + 1) * 2 * COLS)
        out = jnp.dot(kernel, taps[:, cut], preferred_element_type=F32)
        surface = x_ref[r + 1, 64:CPAD, cut].astype(F32)[CIN - 64 : CIN - 63]
        out = gelu_times(out, 0.5 * surface).astype(BF16)
        hb_ref[r, :HID, cut] = pltpu.roll(out, 1, 1)
        hb_ref[r, HID : 2 * HID, cut] = out
        hb_ref[r, 2 * HID :, cut] = pltpu.roll(out, 2 * COLS - 1, 1)


def output_row(x_ref, hb_ref, k2_ref, y_ref, bias, r):
    kernel = jnp.concatenate([k2_ref[t] for t in range(9)], 1)
    taps = hb_ref[r : r + 3].reshape(9 * HID, WIDE)
    column = jnp.bitwise_and(lanes_of((1, 2 * COLS)), COLS - 1)
    inner = jnp.logical_and(column >= 2, column < COLS - 2)
    for pair in range(2):
        cut = slice(pair * 2 * COLS, (pair + 1) * 2 * COLS)
        out = jnp.dot(kernel, taps[:, cut], preferred_element_type=F32)
        surface = x_ref[r + 2, 64:CPAD, cut].astype(F32)[CIN - 64 : CIN - 63]
        surface = jnp.where(inner, surface, 0.0)
        out = ((out + jnp.concatenate([bias] * 4, 1)) * surface).astype(BF16)
        y_ref[r, 2 * pair] = out[:, :COLS]
        y_ref[r, 2 * pair + 1] = out[:, COLS:]


def edge_columns(columns, k1_ref, k2_ref, bias2, top):
    lane = lanes_of((HID, 128))
    back = [[c if not a else pltpu.roll(c, 128 - 8 * a, 1) for a in range(3)] for c in columns]
    taps = jnp.concatenate(
        [jnp.concatenate([back[i + b][a] for a in range(3) for b in range(3)], 0).astype(BF16) for i in range(4)], 1
    )
    plain = jnp.dot(k1_ref[0], taps, preferred_element_type=F32)
    turned = jnp.dot(k1_ref[1], taps, preferred_element_type=F32)
    ghost = lane >= jnp.where(top, 72, 128)
    hidden = []
    for i in range(4):
        cut = slice(i * 128, (i + 1) * 128)
        out = jnp.where(ghost, turned[:, cut], plain[:, cut])
        out = gelu_times(out, 0.5 * back[i + 1][1][CIN : CIN + 1, :])
        hidden.append([out if not a else pltpu.roll(out, 128 - 8 * a, 1) for a in range(3)])
    taps = jnp.concatenate(
        [jnp.concatenate([hidden[i + b][a] for a in range(3) for b in range(3)], 0).astype(BF16) for i in range(2)], 1
    )
    kernel = jnp.concatenate([k2_ref[t] for t in range(9)], 1)
    out = jnp.dot(kernel, taps, preferred_element_type=F32)
    first, second = ((out[:, i * 128 : i * 128 + 128] + bias2) * back[i + 2][2][CIN : CIN + 1, :] for i in range(2))
    even = jnp.bitwise_and(lane, 1) == 0
    return jnp.where(even, first, pltpu.roll(second, 1, 1)), jnp.where(even, pltpu.roll(first, 127, 1), second)


def fold_kernel_parts(a_ref, y0_ref, y1_ref, s_ref, se_ref, fold_ref, lon):
    start = fold_ref[0]
    turn = jnp.bitwise_and(start, COLS - 1)
    block = lax.shift_right_logical(start, 8)
    source = lax.broadcasted_iota(jnp.int32, (COLS, COLS), 0)
    lane = lax.broadcasted_iota(jnp.int32, (COLS, COLS), 1)
    pieces = a_ref[...].reshape(NLON * 48, COLS)
    for y_ref, target in ((y0_ref, turn), (y1_ref, turn + COLS)):
        choose = jnp.where(source + lane == target, 1.0, 0.0).astype(BF16)
        y_ref[...] = jnp.dot(pieces, choose, preferred_element_type=F32).astype(BF16).reshape(NLON, 48, COLS)
    for d in range(NLON):
        b = jnp.bitwise_and(block + lon - d, NLON - 1)
        s_ref[d] = y0_ref[b] + y1_ref[jnp.bitwise_and(b + NLON - 1, NLON - 1)]
    group = lax.shift_right_logical(lane, 4)
    step = jnp.where(group >= 8, group - 16, group)
    k = jnp.bitwise_and(lane, 15)
    column = jnp.where(k < 2, k - 2, k + COLS - 2)
    hit = jnp.logical_and(k < 4, source == turn - column - COLS * step)
    outer = jnp.dot(pieces, jnp.where(hit, 1.0, 0.0).astype(BF16), preferred_element_type=F32).reshape(NLON, 48, COLS)
    total = jnp.zeros((48, COLS), F32)
    for e in range(NLON):
        total = total + pltpu.roll(outer[e], jnp.bitwise_and(16 * (block + lon - e), COLS - 1), 1)
    total = jnp.concatenate([total, jnp.zeros((80, COLS), F32)], 0)
    se_ref[...] = jnp.transpose(total).astype(BF16).reshape(NLON, 16, 128)


def fold_edges(fe_ref):
    sent = jnp.transpose(fe_ref[...].reshape(NLON * 16, 128).astype(F32)).astype(BF16)
    f = lax.broadcasted_iota(jnp.int32, (256, 512), 0)
    lane = lax.broadcasted_iota(jnp.int32, (256, 512), 1)
    to_lane, side, half = jnp.bitwise_and(lane, 127), jnp.bitwise_and(lane // 128, 1), lane // 256
    hit = jnp.logical_and(
        jnp.bitwise_and(f // 16, 1) == half,
        jnp.logical_and(
            jnp.bitwise_and(f, 15) == 2 * side + jnp.bitwise_and(to_lane, 1),
            to_lane // 2 == 40 + (f // 128) * 4 + jnp.bitwise_and(f // 32, 3),
        ),
    )
    got = jnp.dot(sent, jnp.where(hit, 1.0, 0.0).astype(BF16), preferred_element_type=F32)
    return [jnp.concatenate([got[:48, n : n + 128], got[:32, 256 + n : 384 + n]], 0) for n in (0, 128)]


def main_kernel(
    state_hbm, mask_hbm, fold_ref, k1_hbm, b1_ref, k2_hbm, b2_ref, y_hbm, edge_out,
    state_ref, mask_ref, k1_raw, k1_pad, k1_ref, k2_ref, x_ref, t_ref, xb_ref, hb_ref, y_ref,
    sp_ref, lp_ref, rp_ref, relay_ref, a_ref, y0_ref, y1_ref, s_ref, se_ref, fe_ref, ft_ref,
    load_sem, store_sem,
    row_send, row_recv, relay_send, relay_recv, pass_send, pass_recv, edge_send, edge_recv, f1_send, f1_recv, f2_send, f2_recv, f3_send, f3_recv,
):
    loads = [
        pltpu.make_async_copy(src, dst, load_sem.at[n])
        for n, (src, dst) in enumerate(((mask_hbm, mask_ref), (state_hbm, state_ref), (k1_hbm, k1_raw), (k2_hbm, k2_ref)))
    ]
    for load in loads:
        load.start()
    lon = lax.axis_index("lon")
    lat = lax.axis_index("lat")
    right, left = lax.rem(lon + 1, NLON), lax.rem(lon + NLON - 1, NLON)
    top = lat == NLAT - 1
    has = {-1: lat > 0, 0: None, 1: lat < NLAT - 1}

    def when(flag, fn):
        if flag is None:
            fn()
        else:
            pl.when(flag)(fn)

    barrier = pltpu.get_barrier_semaphore()

    def greet(at_lat, at_lon):
        pl.semaphore_signal(barrier, inc=1, device_id={"lat": at_lat, "lon": at_lon}, device_id_type=MESH)

    for d in (-1, 0, 1):
        def hello(d=d):
            if d:
                greet(lat + d, lon)
            greet(lat + d, left)
            greet(lat + d, right)
        when(has[d], hello)

    @pl.when(top)
    def _():
        for k in range(2, NLON - 1):
            greet(lat, lax.rem(lon + k, NLON))

    is_relay, is_low, is_high = lat == 0, lat == NLAT // 2 - 1, lat == NLAT // 2
    pl.when(is_relay)(lambda: [greet(NLAT // 2 - 1, lon), greet(NLAT // 2, lon)] and None)
    pl.when(jnp.logical_or(is_low, is_high))(lambda: greet(0, lon))

    loads[0].wait()
    loads[1].wait()
    prepare(state_ref, mask_ref, x_ref, t_ref)
    pairs = edge_pairs(x_ref, range(2, 2 + ROWS), [jnp.zeros((CPAD, 128), F32)] * 4)
    for n, pair in enumerate((pairs[0], pairs[3])):
        sp_ref[n] = jnp.transpose(jnp.concatenate([pair, jnp.zeros((48, 128), F32)], 0)).astype(BF16)
    loads[2].wait()
    stack_taps(k1_raw, b1_ref, k1_pad, k1_ref, False)
    bias2 = wide_bias(b2_ref)

    def hidden(r, which=0):
        hidden_row(x_ref, xb_ref, hb_ref, k1_ref, which, r)

    stores = []

    def output(r):
        output_row(x_ref, hb_ref, k2_ref, y_ref, bias2, r)
        stores.append(pltpu.make_async_copy(y_ref.at[r], y_hbm.at[:, r], store_sem.at[r]))
        stores[-1].start()

    for r in range(2, 2 + ROWS):
        shift_row(x_ref, xb_ref, r)
    for r in EARLY:
        hidden(r)

    @pl.when(lat == 0)
    def _():
        x_ref[0:2] = jnp.zeros((2, CPAD, WIDE), BF16)
        lp_ref[0:16] = jnp.zeros((16, 128), BF16)
        rp_ref[0:16] = jnp.zeros((16, 128), BF16)

    @pl.when(jnp.logical_or(is_low, is_high))
    def _():
        pl.semaphore_wait(barrier, 9)

    @pl.when(jnp.logical_and(jnp.logical_and(lat > 0, lat < NLAT - 1), jnp.logical_not(jnp.logical_or(is_low, is_high))))
    def _():
        pl.semaphore_wait(barrier, 8)

    @pl.when(lat == 0)
    def _():
        pl.semaphore_wait(barrier, 7)

    @pl.when(top)
    def _():
        pl.semaphore_wait(barrier, 18)

    def to(src, dst, send, recv, at_lat, at_lon):
        return pltpu.make_async_remote_copy(
            src_ref=src, dst_ref=dst, send_sem=send, recv_sem=recv,
            device_id={"lat": at_lat, "lon": at_lon}, device_id_type=MESH,
        )

    def first_copy(i):
        row, s, half = piece(i)
        at, n = HALF[half]
        return to(
            x_ref.at[9 - row, pl.ds(at, n), pl.ds(s * COLS, COLS)], a_ref.at[lon, pl.ds(0, n)],
            f1_send.at[i], f1_recv.at[lon], lat, i,
        )

    my_row, my_s, my_half = piece(lon)

    def second_copy(d, half):
        at, n = HALF[half]
        return to(
            s_ref.at[d, pl.ds(0, n)],
            x_ref.at[10 + my_row, pl.ds(at, n), pl.ds(pl.multiple_of(my_s * COLS, COLS), COLS)],
            f2_send.at[d], f2_recv.at[lon], lat, d,
        )

    def third_copy(d):
        return to(se_ref.at[d], fe_ref.at[lon], f3_send.at[d], f3_recv.at[lon], lat, d)

    up = to(x_ref.at[pl.ds(8, 2)], x_ref.at[pl.ds(0, 2)], row_send.at[0], row_recv.at[0], lat + 1, lon)
    def relay_copy(s):
        return to(
            x_ref.at[pl.ds(2, 2), :, pl.ds(s * COLS, COLS)], relay_ref.at[s],
            relay_send.at[s], relay_recv.at[s], 0, lon,
        )

    def pass_copy(s):
        return to(
            relay_ref.at[s], x_ref.at[pl.ds(10, 2), :, pl.ds(s * COLS, COLS)],
            pass_send.at[s], pass_recv.at[s], NLAT // 2 - 1, lon,
        )

    def hand_on(s):
        @pl.when(is_relay)
        def _():
            relay_copy(s).wait_recv()
            pass_copy(s).start()

    direct = jnp.logical_and(lat > 0, jnp.logical_not(is_high))
    down = to(x_ref.at[pl.ds(2, 2)], x_ref.at[pl.ds(10, 2)], row_send.at[1], row_recv.at[1], lat - 1, lon)
    edge = {}
    for d, at, n, there in ((-1, 16, 16, 80), (0, 16, 64, 16), (1, 64, 16, 0)):
        edge[d] = (
            to(sp_ref.at[0, pl.ds(at, n)], rp_ref.at[pl.ds(there, n)], edge_send.at[d + 1], edge_recv.at[1 - d], lat + d, left),
            to(sp_ref.at[1, pl.ds(at, n)], lp_ref.at[pl.ds(there, n)], edge_send.at[d + 4], edge_recv.at[4 - d], lat + d, right),
        )

    @pl.when(top)
    def _():
        for i in range(NLON):
            pl.when(i != lon)(lambda i=i: first_copy(i).start())

    for d in (-1, 0, 1):
        def go(d=d):
            edge[d][0].start()
            edge[d][1].start()
        when(has[d], go)
    @pl.when(is_high)
    def _():
        for s in range(SAMPLES):
            relay_copy(s).start()

    pl.when(has[1])(lambda: up.start())
    pl.when(direct)(lambda: down.start())

    for r in range(2, HROWS - 2):
        if r not in EARLY:
            hidden(r)
    loads[3].wait()
    output(2)
    output(3)
    hand_on(0)
    output(4)
    hand_on(1)

    @pl.when(top)
    def _():
        for half in (0, 1):
            at, n = HALF[half]

            @pl.when(my_half == half)
            def _():
                mine = x_ref.at[9 - my_row, pl.ds(at, n), pl.ds(pl.multiple_of(my_s * COLS, COLS), COLS)]
                a_ref[lon, 0:n] = mine[...]
                if n < 48:
                    a_ref[:, n:] = jnp.zeros((NLON, 48 - n, COLS), BF16)
                for e in range(NLON):
                    def arrive(e=e):
                        to(a_ref.at[e, pl.ds(0, n)], a_ref.at[e, pl.ds(0, n)], f1_send.at[e], f1_recv.at[e], lat, e).wait_recv()
                    pl.when(e != lon)(arrive)

        fold_kernel_parts(a_ref, y0_ref, y1_ref, s_ref, se_ref, fold_ref, lon)
        for half in (0, 1):
            at, n = HALF[half]

            @pl.when(my_half == half)
            def _():
                for d in range(NLON):
                    pl.when(d != lon)(lambda d=d: second_copy(d, half).start())
                x_ref[10 + my_row, at : at + n, pl.ds(pl.multiple_of(my_s * COLS, COLS), COLS)] = s_ref[lon, 0:n]
        for d in range(NLON):
            pl.when(d != lon)(lambda d=d: third_copy(d).start())
        fe_ref[lon] = se_ref[lon]

    output(5)
    hand_on(2)

    @pl.when(top)
    def _():
        stack_taps(k1_raw, b1_ref, k1_pad, k1_ref, True)

    pl.when(has[-1])(lambda: up.wait_recv())
    shift_row(x_ref, xb_ref, 0)
    shift_row(x_ref, xb_ref, 1)
    hidden(1)
    hidden(0)
    hand_on(3)
    output(1)
    output(0)

    pl.when(jnp.logical_and(has[1], jnp.logical_not(is_low)))(lambda: down.wait_recv())

    @pl.when(is_low)
    def _():
        for s in range(SAMPLES):
            pass_copy(s).wait_recv()

    @pl.when(top)
    def _():
        for e in range(NLON):
            row, s, half = piece(e)
            at, n = HALF[half]
            def arrive(e=e, row=row, s=s, at=at, n=n):
                there = x_ref.at[10 + row, pl.ds(at, n), pl.ds(s * COLS, COLS)]
                to(there, there, f2_send.at[e], f2_recv.at[e], lat, e).wait_recv()
                to(fe_ref.at[e], fe_ref.at[e], f3_send.at[e], f3_recv.at[e], lat, e).wait_recv()
            pl.when(e != lon)(arrive)
        for n, part in enumerate(fold_edges(fe_ref)):
            ft_ref[n] = part

    shift_row(x_ref, xb_ref, ROWS + 2)
    shift_row(x_ref, xb_ref, ROWS + 3)
    hidden(ROWS)
    hidden(ROWS + 1, jnp.where(top, 1, 0))
    output(6)
    output(7)

    for d in (-1, 0, 1):
        def got(d=d):
            edge[-d][0].wait_recv()
            edge[-d][1].wait_recv()
        when(has[d], got)
    pairs = edge_pairs(x_ref, (0, 1, 10, 11), pairs)
    lane = lanes_of((CPAD, 128))

    def joined(ref, n):
        sent = jnp.transpose(ref[...].astype(F32))[:CPAD]
        return jnp.where(jnp.logical_and(top, lane >= 80), ft_ref[n], sent)

    before, after = joined(lp_ref, 0), joined(rp_ref, 1)
    even = jnp.bitwise_and(lane, 1) == 0
    columns = []
    for low, high in ((before, pairs[2]), (pairs[0], pairs[3]), (pairs[1], after)):
        columns.append(jnp.where(even, low, pltpu.roll(high, 1, 1)))
        columns.append(jnp.where(even, pltpu.roll(low, 127, 1), high))
    first, last = edge_columns(columns, k1_ref, k2_ref, bias2, top)
    used = lanes_of((HID, 128)) < 64
    edge_out[0] = jnp.where(used, first, 0.0).astype(BF16)
    edge_out[1] = jnp.where(used, last, 0.0).astype(BF16)

    pl.when(has[1])(lambda: up.wait_send())
    pl.when(direct)(lambda: down.wait_send())

    @pl.when(is_high)
    def _():
        for s in range(SAMPLES):
            relay_copy(s).wait_send()

    @pl.when(is_relay)
    def _():
        for s in range(SAMPLES):
            pass_copy(s).wait_send()

    for d in (-1, 0, 1):
        def sent(d=d):
            edge[d][0].wait_send()
            edge[d][1].wait_send()
        when(has[d], sent)

    @pl.when(top)
    def _():
        for i in range(NLON):
            pl.when(i != lon)(lambda i=i: first_copy(i).wait_send())
        for half in (0, 1):
            @pl.when(my_half == half)
            def _():
                for d in range(NLON):
                    pl.when(d != lon)(lambda d=d: second_copy(d, half).wait_send())
        for d in range(NLON):
            pl.when(d != lon)(lambda d=d: third_copy(d).wait_send())
    for store in stores:
        store.wait()


HBM = pl.BlockSpec(memory_space=pl.ANY)


def main(state, mask, fold, k1, b1, k2, b2):
    dma = pltpu.SemaphoreType.DMA
    return pl.pallas_call(
        main_kernel,
        out_shape=(
            jax.ShapeDtypeStruct((SAMPLES, ROWS, HID, COLS), BF16),
            jax.ShapeDtypeStruct((2, HID, 128), BF16),
        ),
        in_specs=[HBM, HBM, SMEM, HBM, VMEM, HBM, VMEM],
        out_specs=(HBM, VMEM),
        scratch_shapes=[
            pltpu.VMEM(state.shape, BF16),
            pltpu.VMEM(mask.shape, jnp.int32),
            pltpu.VMEM(k1.shape, BF16),
            pltpu.VMEM((6 * 128, HID), F32),
            pltpu.VMEM((2, HID, 9 * CPAD), BF16),
            pltpu.VMEM(k2.shape, BF16),
            pltpu.VMEM((XROWS, CPAD, WIDE), BF16),
            pltpu.VMEM((SAMPLES, 2, CPAD * ROWS, 128), F32),
            pltpu.VMEM((XROWS, 3 * CPAD, WIDE), BF16),
            pltpu.VMEM((HROWS, 3 * HID, WIDE), BF16),
            pltpu.VMEM((ROWS, SAMPLES, HID, COLS), BF16),
            pltpu.VMEM((2, 128, 128), BF16),
            pltpu.VMEM((128, 128), BF16),
            pltpu.VMEM((128, 128), BF16),
            pltpu.VMEM((SAMPLES, 2, CPAD, COLS), BF16),
            pltpu.VMEM((NLON, 48, COLS), BF16),
            pltpu.VMEM((NLON, 48, COLS), BF16),
            pltpu.VMEM((NLON, 48, COLS), BF16),
            pltpu.VMEM((NLON, 48, COLS), BF16),
            pltpu.VMEM((NLON, 16, 128), BF16),
            pltpu.VMEM((NLON, 16, 128), BF16),
            pltpu.VMEM((2, CPAD, 128), F32),
            dma((4,)), dma((ROWS,)),
            dma((2,)), dma((2,)), dma((SAMPLES,)), dma((SAMPLES,)), dma((SAMPLES,)), dma((SAMPLES,)), dma((6,)), dma((6,)),
            dma((NLON,)), dma((NLON,)), dma((NLON,)), dma((NLON,)), dma((NLON,)), dma((NLON,)),
        ],
        compiler_params=pltpu.CompilerParams(collective_id=0, has_side_effects=True, vmem_limit_bytes=LIMIT),
    )(state, mask, fold, k1, b1, k2, b2)


CHANNELS = 128
AHEAD = 8
CHUNKS = [(s, c) for s in range(SAMPLES) for c in range(HID // CHANNELS)]


def order_kernel(y_hbm, edge_ref, out_hbm, y_ref, out_ref, load_sem, store_sem):
    loads, stores = [], []
    for n, (s, c) in enumerate(CHUNKS):
        part = pl.ds(c * CHANNELS, CHANNELS)
        loads.append(pltpu.make_async_copy(y_hbm.at[s, :, part], y_ref.at[n], load_sem.at[n]))
        stores.append(pltpu.make_async_copy(out_ref.at[n], out_hbm.at[s, part], store_sem.at[n]))
    for load in loads[:AHEAD]:
        load.start()
    lane = lanes_of((CHANNELS, 128))
    at_first = jnp.where(lane < 2, 1.0, 0.0).astype(BF16)
    at_last = jnp.where(lane >= 126, 1.0, 0.0).astype(BF16)
    for n, (s, c) in enumerate(CHUNKS):
        cut = slice(c * CHANNELS, (c + 1) * CHANNELS)
        first, last = edge_ref[0, cut], edge_ref[1, cut]
        loads[n].wait()
        if n + AHEAD < len(loads):
            loads[n + AHEAD].start()
        for r in range(ROWS):
            at = 8 * r + 2 * s
            low = at_first * (pltpu.roll(first, 128 - at, 1) if at else first)
            high = at_last * pltpu.roll(last, 126 - at, 1)
            y_ref[n, r, :, :128] = y_ref[n, r, :, :128] + low
            y_ref[n, r, :, 128:] = y_ref[n, r, :, 128:] + high
        out_ref[n] = jnp.swapaxes(y_ref[n], 0, 1)
        stores[n].start()
    for store in stores:
        store.wait()


def order(y, edges):
    return pl.pallas_call(
        order_kernel,
        out_shape=jax.ShapeDtypeStruct((SAMPLES, HID, ROWS, COLS), BF16),
        in_specs=[HBM, VMEM],
        out_specs=HBM,
        scratch_shapes=[
            pltpu.VMEM((len(CHUNKS), ROWS, CHANNELS, COLS), BF16),
            pltpu.VMEM((len(CHUNKS), CHANNELS, ROWS, COLS), BF16),
            pltpu.SemaphoreType.DMA((len(CHUNKS),)),
            pltpu.SemaphoreType.DMA((len(CHUNKS),)),
        ],
        compiler_params=pltpu.CompilerParams(vmem_limit_bytes=LIMIT),
    )(y, edges)


def on_device(state, mask, fold, first_kernel, first_bias, second_kernel, second_bias):
    y, edges = main(state, mask, fold, jnp.transpose(first_kernel, (0, 2, 1)), first_bias[None], second_kernel, second_bias[None])
    return order(y, edges)


def solution(mesh):
    return jax.shard_map(
        on_device,
        mesh=mesh,
        in_specs=(P(None, None, "lat", "lon"), P(None, "lat", "lon"), P("lon"), P(), P(), P(), P()),
        out_specs=P(None, None, "lat", "lon"),
        check_vma=False,
    )
```

```python
import functools

import jax
import jax.numpy as jnp
from jax import lax
from jax.experimental import pallas as pl
from jax.experimental.pallas import tpu as pltpu
from jax.sharding import PartitionSpec as P

F32 = jnp.float32
BF16 = jnp.bfloat16
MESH = pl.DeviceIdType.MESH
VMEM = pl.BlockSpec(memory_space=pltpu.VMEM)
SMEM = pl.BlockSpec(memory_space=pltpu.SMEM)

SAMPLES, CIN, ROWS, COLS, HID = 4, 75, 8, 256, 256
CPAD = 80
WIDE = SAMPLES * COLS
XROWS = ROWS + 4
HROWS = ROWS + 2
NLON, NLAT = 16, 8
LIMIT = 60 * 1024 * 1024


def lanes_of(shape):
    return lax.broadcasted_iota(jnp.int32, shape, len(shape) - 1)


def edge_pairs(x_ref, rows, pairs):
    pair = lax.shift_right_logical(lanes_of((CPAD, 128)), 1)
    pairs = list(pairs)
    for r in rows:
        for s in range(SAMPLES):
            row = x_ref[r, :, s * COLS : (s + 1) * COLS].astype(F32)
            at = 8 * r + 2 * s
            here = pair == at // 2
            for n, (half, by) in enumerate(((0, at), (0, at - 2), (1, at + 4), (1, at + 2))):
                part = pltpu.roll(row[:, half * 128 : half * 128 + 128], by % 128, 1)
                pairs[n] = jnp.where(here, part, pairs[n])
    return pairs


def prepare(state_ref, mask_ref, x_ref, t_ref):
    for s in range(SAMPLES):
        for h in range(2):
            cut = slice(h * 128, (h + 1) * 128)
            t_ref[s, h, CIN * ROWS : (CIN + 1) * ROWS, :] = mask_ref[0, :, cut].astype(F32)
            t_ref[s, h, (CIN + 1) * ROWS : (CIN + 4) * ROWS, :] = jnp.ones((3 * ROWS, 128), F32)
            t_ref[s, h, (CIN + 4) * ROWS :, :] = jnp.zeros(((CPAD - CIN - 4) * ROWS, 128), F32)
            masked = state_ref[s, :, :, cut].astype(F32) * mask_ref[:, :, cut].astype(F32)
            t_ref[s, h, : CIN * ROWS, :] = masked.reshape(CIN * ROWS, 128)
            for r in range(ROWS):
                at = s * COLS + h * 128
                x_ref[r + 2, :, at : at + 128] = t_ref[s, h, pl.ds(r, CPAD, stride=ROWS), :].astype(BF16)


def piece(i):
    return i // 8, (i // 2) % 4, i % 2


HALF = ((0, 48), (48, 32))


def gelu_times(x, half_surface):
    half = x * half_surface
    return half + half * jnp.tanh(x * (0.7978845608028654 + 0.035677408136300125 * (x * x)))


def wide_bias(ref):
    return jnp.transpose(jnp.broadcast_to(ref[...], (128, HID)))


def stack_taps(raw_ref, bias_ref, pad_ref, k1_ref, turned):
    pad_ref[9 * CPAD :, :] = jnp.zeros((pad_ref.shape[0] - 9 * CPAD, HID), F32)
    for t in range(9):
        at = CPAD * (8 - t if turned else t)
        pad_ref[at + 72 : at + CPAD, :] = jnp.zeros((8, HID), F32)
        pad_ref[at : at + CIN, :] = raw_ref[t].astype(F32)
    at = 4 * CPAD + CIN + 1
    rest = bias_ref[...]
    for n in range(3):
        part = rest.astype(BF16).astype(F32)
        pad_ref[at + n : at + n + 1, :] = part
        rest = rest - part
    k1_ref[1 if turned else 0] = jnp.transpose(pad_ref[...])[:, : 9 * CPAD].astype(BF16)


def shift_row(x_ref, xb_ref, r):
    row = x_ref[r]
    xb_ref[r, :CPAD, :] = pltpu.roll(row, 1, 1)
    xb_ref[r, CPAD : 2 * CPAD, :] = row
    xb_ref[r, 2 * CPAD :, :] = pltpu.roll(row, WIDE - 1, 1)


def hidden_row(x_ref, xb_ref, hb_ref, k1_ref, which, r):
    kernel = k1_ref[which]
    taps = xb_ref[r : r + 3].reshape(9 * CPAD, WIDE)
    for pair in range(2):
        cut = slice(pair * 2 * COLS, (pair + 1) * 2 * COLS)
        out = jnp.dot(kernel, taps[:, cut], preferred_element_type=F32)
        surface = x_ref[r + 1, 64:CPAD, cut].astype(F32)[CIN - 64 : CIN - 63]
        out = gelu_times(out, 0.5 * surface).astype(BF16)
        hb_ref[r, :HID, cut] = pltpu.roll(out, 1, 1)
        hb_ref[r, HID : 2 * HID, cut] = out
        hb_ref[r, 2 * HID :, cut] = pltpu.roll(out, 2 * COLS - 1, 1)


def output_row(x_ref, hb_ref, k2_ref, y_ref, bias, r):
    kernel = jnp.concatenate([k2_ref[t] for t in range(9)], 1)
    taps = hb_ref[r : r + 3].reshape(9 * HID, WIDE)
    column = jnp.bitwise_and(lanes_of((1, 2 * COLS)), COLS - 1)
    inner = jnp.logical_and(column >= 2, column < COLS - 2)
    for pair in range(2):
        cut = slice(pair * 2 * COLS, (pair + 1) * 2 * COLS)
        out = jnp.dot(kernel, taps[:, cut], preferred_element_type=F32)
        surface = x_ref[r + 2, 64:CPAD, cut].astype(F32)[CIN - 64 : CIN - 63]
        surface = jnp.where(inner, surface, 0.0)
        out = ((out + jnp.concatenate([bias] * 4, 1)) * surface).astype(BF16)
        y_ref[r, 2 * pair] = out[:, :COLS]
        y_ref[r, 2 * pair + 1] = out[:, COLS:]


def edge_columns(columns, k1_ref, k2_ref, bias2, top):
    lane = lanes_of((HID, 128))
    back = [[c if not a else pltpu.roll(c, 128 - 8 * a, 1) for a in range(3)] for c in columns]
    taps = jnp.concatenate(
        [jnp.concatenate([back[i + b][a] for a in range(3) for b in range(3)], 0).astype(BF16) for i in range(4)], 1
    )
    plain = jnp.dot(k1_ref[0], taps, preferred_element_type=F32)
    turned = jnp.dot(k1_ref[1], taps, preferred_element_type=F32)
    ghost = lane >= jnp.where(top, 72, 128)
    hidden = []
    for i in range(4):
        cut = slice(i * 128, (i + 1) * 128)
        out = jnp.where(ghost, turned[:, cut], plain[:, cut])
        out = gelu_times(out, 0.5 * back[i + 1][1][CIN : CIN + 1, :])
        hidden.append([out if not a else pltpu.roll(out, 128 - 8 * a, 1) for a in range(3)])
    taps = jnp.concatenate(
        [jnp.concatenate([hidden[i + b][a] for a in range(3) for b in range(3)], 0).astype(BF16) for i in range(2)], 1
    )
    kernel = jnp.concatenate([k2_ref[t] for t in range(9)], 1)
    out = jnp.dot(kernel, taps, preferred_element_type=F32)
    first, second = ((out[:, i * 128 : i * 128 + 128] + bias2) * back[i + 2][2][CIN : CIN + 1, :] for i in range(2))
    even = jnp.bitwise_and(lane, 1) == 0
    return jnp.where(even, first, pltpu.roll(second, 1, 1)), jnp.where(even, pltpu.roll(first, 127, 1), second)


def fold_kernel_parts(a_ref, y0_ref, y1_ref, s_ref, se_ref, fold_ref, lon):
    start = fold_ref[0]
    turn = jnp.bitwise_and(start, COLS - 1)
    block = lax.shift_right_logical(start, 8)
    source = lax.broadcasted_iota(jnp.int32, (COLS, COLS), 0)
    lane = lax.broadcasted_iota(jnp.int32, (COLS, COLS), 1)
    pieces = a_ref[...].reshape(NLON * 48, COLS)
    for y_ref, target in ((y0_ref, turn), (y1_ref, turn + COLS)):
        choose = jnp.where(source + lane == target, 1.0, 0.0).astype(BF16)
        y_ref[...] = jnp.dot(pieces, choose, preferred_element_type=F32).astype(BF16).reshape(NLON, 48, COLS)
    for d in range(NLON):
        b = jnp.bitwise_and(block + lon - d, NLON - 1)
        s_ref[d] = y0_ref[b] + y1_ref[jnp.bitwise_and(b + NLON - 1, NLON - 1)]
    group = lax.shift_right_logical(lane, 4)
    step = jnp.where(group >= 8, group - 16, group)
    k = jnp.bitwise_and(lane, 15)
    column = jnp.where(k < 2, k - 2, k + COLS - 2)
    hit = jnp.logical_and(k < 4, source == turn - column - COLS * step)
    outer = jnp.dot(pieces, jnp.where(hit, 1.0, 0.0).astype(BF16), preferred_element_type=F32).reshape(NLON, 48, COLS)
    total = jnp.zeros((48, COLS), F32)
    for e in range(NLON):
        total = total + pltpu.roll(outer[e], jnp.bitwise_and(16 * (block + lon - e), COLS - 1), 1)
    total = jnp.concatenate([total, jnp.zeros((80, COLS), F32)], 0)
    se_ref[...] = jnp.transpose(total).astype(BF16).reshape(NLON, 16, 128)


def fold_edges(fe_ref):
    sent = jnp.transpose(fe_ref[...].reshape(NLON * 16, 128).astype(F32)).astype(BF16)
    f = lax.broadcasted_iota(jnp.int32, (256, 512), 0)
    lane = lax.broadcasted_iota(jnp.int32, (256, 512), 1)
    to_lane, side, half = jnp.bitwise_and(lane, 127), jnp.bitwise_and(lane // 128, 1), lane // 256
    hit = jnp.logical_and(
        jnp.bitwise_and(f // 16, 1) == half,
        jnp.logical_and(
            jnp.bitwise_and(f, 15) == 2 * side + jnp.bitwise_and(to_lane, 1),
            to_lane // 2 == 40 + (f // 128) * 4 + jnp.bitwise_and(f // 32, 3),
        ),
    )
    got = jnp.dot(sent, jnp.where(hit, 1.0, 0.0).astype(BF16), preferred_element_type=F32)
    return [jnp.concatenate([got[:48, n : n + 128], got[:32, 256 + n : 384 + n]], 0) for n in (0, 128)]


def main_kernel(
    state_hbm, mask_hbm, fold_ref, k1_hbm, b1_ref, k2_hbm, b2_ref, y_hbm, edge_out,
    state_ref, mask_ref, k1_raw, k1_pad, k1_ref, k2_ref, x_ref, t_ref, xb_ref, hb_ref, y_ref,
    sp_ref, lp_ref, rp_ref, relay_ref, a_ref, y0_ref, y1_ref, s_ref, se_ref, fe_ref, ft_ref,
    load_sem, store_sem,
    row_send, row_recv, relay_send, relay_recv, pass_send, pass_recv, edge_send, edge_recv, f1_send, f1_recv, f2_send, f2_recv, f3_send, f3_recv,
):
    loads = [
        pltpu.make_async_copy(src, dst, load_sem.at[n])
        for n, (src, dst) in enumerate(((mask_hbm, mask_ref), (state_hbm, state_ref), (k1_hbm, k1_raw), (k2_hbm, k2_ref)))
    ]
    for load in loads:
        load.start()
    lon = lax.axis_index("lon")
    lat = lax.axis_index("lat")
    right, left = lax.rem(lon + 1, NLON), lax.rem(lon + NLON - 1, NLON)
    top = lat == NLAT - 1
    has = {-1: lat > 0, 0: None, 1: lat < NLAT - 1}

    def when(flag, fn):
        if flag is None:
            fn()
        else:
            pl.when(flag)(fn)

    barrier = pltpu.get_barrier_semaphore()

    def greet(at_lat, at_lon):
        pl.semaphore_signal(barrier, inc=1, device_id={"lat": at_lat, "lon": at_lon}, device_id_type=MESH)

    for d in (-1, 0, 1):
        def hello(d=d):
            if d:
                greet(lat + d, lon)
            greet(lat + d, left)
            greet(lat + d, right)
        when(has[d], hello)

    @pl.when(top)
    def _():
        for k in range(2, NLON - 1):
            greet(lat, lax.rem(lon + k, NLON))

    is_relay, is_low, is_high = lat == 0, lat == NLAT // 2 - 1, lat == NLAT // 2
    pl.when(is_relay)(lambda: [greet(NLAT // 2 - 1, lon), greet(NLAT // 2, lon)] and None)
    pl.when(jnp.logical_or(is_low, is_high))(lambda: greet(0, lon))

    loads[0].wait()
    loads[1].wait()
    prepare(state_ref, mask_ref, x_ref, t_ref)

    def hidden(r, which=0):
        hidden_row(x_ref, xb_ref, hb_ref, k1_ref, which, r)

    stores = []

    def output(r):
        output_row(x_ref, hb_ref, k2_ref, y_ref, bias2, r)
        stores.append(pltpu.make_async_copy(y_ref.at[r], y_hbm.at[:, r], store_sem.at[r]))
        stores[-1].start()

    @pl.when(lat == 0)
    def _():
        x_ref[0:2] = jnp.zeros((2, CPAD, WIDE), BF16)
        lp_ref[0:16] = jnp.zeros((16, 128), BF16)
        rp_ref[0:16] = jnp.zeros((16, 128), BF16)

    @pl.when(jnp.logical_or(is_low, is_high))
    def _():
        pl.semaphore_wait(barrier, 9)

    @pl.when(jnp.logical_and(jnp.logical_and(lat > 0, lat < NLAT - 1), jnp.logical_not(jnp.logical_or(is_low, is_high))))
    def _():
        pl.semaphore_wait(barrier, 8)

    @pl.when(lat == 0)
    def _():
        pl.semaphore_wait(barrier, 7)

    @pl.when(top)
    def _():
        pl.semaphore_wait(barrier, 18)

    def to(src, dst, send, recv, at_lat, at_lon):
        return pltpu.make_async_remote_copy(
            src_ref=src, dst_ref=dst, send_sem=send, recv_sem=recv,
            device_id={"lat": at_lat, "lon": at_lon}, device_id_type=MESH,
        )

    def first_copy(i):
        row, s, half = piece(i)
        at, n = HALF[half]
        return to(
            x_ref.at[9 - row, pl.ds(at, n), pl.ds(s * COLS, COLS)], a_ref.at[lon, pl.ds(0, n)],
            f1_send.at[i], f1_recv.at[lon], lat, i,
        )

    my_row, my_s, my_half = piece(lon)

    def second_copy(d, half):
        at, n = HALF[half]
        return to(
            s_ref.at[d, pl.ds(0, n)],
            x_ref.at[10 + my_row, pl.ds(at, n), pl.ds(pl.multiple_of(my_s * COLS, COLS), COLS)],
            f2_send.at[d], f2_recv.at[lon], lat, d,
        )

    def third_copy(d):
        return to(se_ref.at[d], fe_ref.at[lon], f3_send.at[d], f3_recv.at[lon], lat, d)

    up = to(x_ref.at[pl.ds(8, 2)], x_ref.at[pl.ds(0, 2)], row_send.at[0], row_recv.at[0], lat + 1, lon)
    def relay_copy(s):
        return to(
            x_ref.at[pl.ds(2, 2), :, pl.ds(s * COLS, COLS)], relay_ref.at[s],
            relay_send.at[s], relay_recv.at[s], 0, lon,
        )

    def pass_copy(s):
        return to(
            relay_ref.at[s], x_ref.at[pl.ds(10, 2), :, pl.ds(s * COLS, COLS)],
            pass_send.at[s], pass_recv.at[s], NLAT // 2 - 1, lon,
        )

    def hand_on(s):
        @pl.when(is_relay)
        def _():
            relay_copy(s).wait_recv()
            pass_copy(s).start()

    direct = jnp.logical_and(lat > 0, jnp.logical_not(is_high))
    down = to(x_ref.at[pl.ds(2, 2)], x_ref.at[pl.ds(10, 2)], row_send.at[1], row_recv.at[1], lat - 1, lon)
    edge = {}
    for d, at, n, there in ((-1, 16, 16, 80), (0, 16, 64, 16), (1, 64, 16, 0)):
        edge[d] = (
            to(sp_ref.at[0, pl.ds(at, n)], rp_ref.at[pl.ds(there, n)], edge_send.at[d + 1], edge_recv.at[1 - d], lat + d, left),
            to(sp_ref.at[1, pl.ds(at, n)], lp_ref.at[pl.ds(there, n)], edge_send.at[d + 4], edge_recv.at[4 - d], lat + d, right),
        )

    @pl.when(top)
    def _():
        for i in range(NLON):
            pl.when(i != lon)(lambda i=i: first_copy(i).start())

    @pl.when(is_high)
    def _():
        for s in range(SAMPLES):
            relay_copy(s).start()

    pl.when(has[1])(lambda: up.start())
    pl.when(direct)(lambda: down.start())
    pairs = edge_pairs(x_ref, range(2, 2 + ROWS), [jnp.zeros((CPAD, 128), F32)] * 4)
    for n, pair in enumerate((pairs[0], pairs[3])):
        sp_ref[n] = jnp.transpose(jnp.concatenate([pair, jnp.zeros((48, 128), F32)], 0)).astype(BF16)
    for d in (-1, 0, 1):
        def go(d=d):
            edge[d][0].start()
            edge[d][1].start()
        when(has[d], go)
    loads[2].wait()
    stack_taps(k1_raw, b1_ref, k1_pad, k1_ref, False)
    bias2 = wide_bias(b2_ref)
    for r in range(2, 2 + ROWS):
        shift_row(x_ref, xb_ref, r)

    for r in range(2, HROWS - 2):
        hidden(r)
    loads[3].wait()
    output(2)

    @pl.when(top)
    def _():
        for half in (0, 1):
            at, n = HALF[half]

            @pl.when(my_half == half)
            def _():
                mine = x_ref.at[9 - my_row, pl.ds(at, n), pl.ds(pl.multiple_of(my_s * COLS, COLS), COLS)]
                a_ref[lon, 0:n] = mine[...]
                if n < 48:
                    a_ref[:, n:] = jnp.zeros((NLON, 48 - n, COLS), BF16)
                for e in range(NLON):
                    def arrive(e=e):
                        to(a_ref.at[e, pl.ds(0, n)], a_ref.at[e, pl.ds(0, n)], f1_send.at[e], f1_recv.at[e], lat, e).wait_recv()
                    pl.when(e != lon)(arrive)

        fold_kernel_parts(a_ref, y0_ref, y1_ref, s_ref, se_ref, fold_ref, lon)
        for half in (0, 1):
            at, n = HALF[half]

            @pl.when(my_half == half)
            def _():
                for d in range(NLON):
                    pl.when(d != lon)(lambda d=d: second_copy(d, half).start())
                x_ref[10 + my_row, at : at + n, pl.ds(pl.multiple_of(my_s * COLS, COLS), COLS)] = s_ref[lon, 0:n]
        for d in range(NLON):
            pl.when(d != lon)(lambda d=d: third_copy(d).start())
        fe_ref[lon] = se_ref[lon]

    hand_on(0)
    output(3)
    hand_on(1)
    output(4)
    hand_on(2)
    output(5)

    @pl.when(top)
    def _():
        stack_taps(k1_raw, b1_ref, k1_pad, k1_ref, True)

    pl.when(has[-1])(lambda: up.wait_recv())
    shift_row(x_ref, xb_ref, 0)
    shift_row(x_ref, xb_ref, 1)
    hand_on(3)
    hidden(1)
    hidden(0)
    output(1)
    output(0)

    pl.when(jnp.logical_and(has[1], jnp.logical_not(is_low)))(lambda: down.wait_recv())

    @pl.when(is_low)
    def _():
        for s in range(SAMPLES):
            pass_copy(s).wait_recv()

    @pl.when(top)
    def _():
        for e in range(NLON):
            row, s, half = piece(e)
            at, n = HALF[half]
            def arrive(e=e, row=row, s=s, at=at, n=n):
                there = x_ref.at[10 + row, pl.ds(at, n), pl.ds(s * COLS, COLS)]
                to(there, there, f2_send.at[e], f2_recv.at[e], lat, e).wait_recv()
                to(fe_ref.at[e], fe_ref.at[e], f3_send.at[e], f3_recv.at[e], lat, e).wait_recv()
            pl.when(e != lon)(arrive)
        for n, part in enumerate(fold_edges(fe_ref)):
            ft_ref[n] = part

    shift_row(x_ref, xb_ref, ROWS + 2)
    shift_row(x_ref, xb_ref, ROWS + 3)
    hidden(ROWS)
    hidden(ROWS + 1, jnp.where(top, 1, 0))
    output(6)
    output(7)

    for d in (-1, 0, 1):
        def got(d=d):
            edge[-d][0].wait_recv()
            edge[-d][1].wait_recv()
        when(has[d], got)
    pairs = edge_pairs(x_ref, (0, 1, 10, 11), pairs)
    lane = lanes_of((CPAD, 128))

    def joined(ref, n):
        sent = jnp.transpose(ref[...].astype(F32))[:CPAD]
        return jnp.where(jnp.logical_and(top, lane >= 80), ft_ref[n], sent)

    before, after = joined(lp_ref, 0), joined(rp_ref, 1)
    even = jnp.bitwise_and(lane, 1) == 0
    columns = []
    for low, high in ((before, pairs[2]), (pairs[0], pairs[3]), (pairs[1], after)):
        columns.append(jnp.where(even, low, pltpu.roll(high, 1, 1)))
        columns.append(jnp.where(even, pltpu.roll(low, 127, 1), high))
    first, last = edge_columns(columns, k1_ref, k2_ref, bias2, top)
    used = lanes_of((HID, 128)) < 64
    edge_out[0] = jnp.where(used, first, 0.0).astype(BF16)
    edge_out[1] = jnp.where(used, last, 0.0).astype(BF16)

    pl.when(has[1])(lambda: up.wait_send())
    pl.when(direct)(lambda: down.wait_send())

    @pl.when(is_high)
    def _():
        for s in range(SAMPLES):
            relay_copy(s).wait_send()

    @pl.when(is_relay)
    def _():
        for s in range(SAMPLES):
            pass_copy(s).wait_send()

    for d in (-1, 0, 1):
        def sent(d=d):
            edge[d][0].wait_send()
            edge[d][1].wait_send()
        when(has[d], sent)

    @pl.when(top)
    def _():
        for i in range(NLON):
            pl.when(i != lon)(lambda i=i: first_copy(i).wait_send())
        for half in (0, 1):
            @pl.when(my_half == half)
            def _():
                for d in range(NLON):
                    pl.when(d != lon)(lambda d=d: second_copy(d, half).wait_send())
        for d in range(NLON):
            pl.when(d != lon)(lambda d=d: third_copy(d).wait_send())
    for store in stores:
        store.wait()


HBM = pl.BlockSpec(memory_space=pl.ANY)


def main(state, mask, fold, k1, b1, k2, b2):
    dma = pltpu.SemaphoreType.DMA
    return pl.pallas_call(
        main_kernel,
        out_shape=(
            jax.ShapeDtypeStruct((SAMPLES, ROWS, HID, COLS), BF16),
            jax.ShapeDtypeStruct((2, HID, 128), BF16),
        ),
        in_specs=[HBM, HBM, SMEM, HBM, VMEM, HBM, VMEM],
        out_specs=(HBM, VMEM),
        scratch_shapes=[
            pltpu.VMEM(state.shape, BF16),
            pltpu.VMEM(mask.shape, jnp.int32),
            pltpu.VMEM(k1.shape, BF16),
            pltpu.VMEM((6 * 128, HID), F32),
            pltpu.VMEM((2, HID, 9 * CPAD), BF16),
            pltpu.VMEM(k2.shape, BF16),
            pltpu.VMEM((XROWS, CPAD, WIDE), BF16),
            pltpu.VMEM((SAMPLES, 2, CPAD * ROWS, 128), F32),
            pltpu.VMEM((XROWS, 3 * CPAD, WIDE), BF16),
            pltpu.VMEM((HROWS, 3 * HID, WIDE), BF16),
            pltpu.VMEM((ROWS, SAMPLES, HID, COLS), BF16),
            pltpu.VMEM((2, 128, 128), BF16),
            pltpu.VMEM((128, 128), BF16),
            pltpu.VMEM((128, 128), BF16),
            pltpu.VMEM((SAMPLES, 2, CPAD, COLS), BF16),
            pltpu.VMEM((NLON, 48, COLS), BF16),
            pltpu.VMEM((NLON, 48, COLS), BF16),
            pltpu.VMEM((NLON, 48, COLS), BF16),
            pltpu.VMEM((NLON, 48, COLS), BF16),
            pltpu.VMEM((NLON, 16, 128), BF16),
            pltpu.VMEM((NLON, 16, 128), BF16),
            pltpu.VMEM((2, CPAD, 128), F32),
            dma((4,)), dma((ROWS,)),
            dma((2,)), dma((2,)), dma((SAMPLES,)), dma((SAMPLES,)), dma((SAMPLES,)), dma((SAMPLES,)), dma((6,)), dma((6,)),
            dma((NLON,)), dma((NLON,)), dma((NLON,)), dma((NLON,)), dma((NLON,)), dma((NLON,)),
        ],
        compiler_params=pltpu.CompilerParams(collective_id=0, has_side_effects=True, vmem_limit_bytes=LIMIT),
    )(state, mask, fold, k1, b1, k2, b2)


CHANNELS = 128
AHEAD = 8
CHUNKS = [(s, c) for s in range(SAMPLES) for c in range(HID // CHANNELS)]


def order_kernel(y_hbm, edge_ref, out_hbm, y_ref, out_ref, load_sem, store_sem):
    loads, stores = [], []
    for n, (s, c) in enumerate(CHUNKS):
        part = pl.ds(c * CHANNELS, CHANNELS)
        loads.append(pltpu.make_async_copy(y_hbm.at[s, :, part], y_ref.at[n], load_sem.at[n]))
        stores.append(pltpu.make_async_copy(out_ref.at[n], out_hbm.at[s, part], store_sem.at[n]))
    for load in loads[:AHEAD]:
        load.start()
    lane = lanes_of((CHANNELS, 128))
    at_first = jnp.where(lane < 2, 1.0, 0.0).astype(BF16)
    at_last = jnp.where(lane >= 126, 1.0, 0.0).astype(BF16)
    for n, (s, c) in enumerate(CHUNKS):
        cut = slice(c * CHANNELS, (c + 1) * CHANNELS)
        first, last = edge_ref[0, cut], edge_ref[1, cut]
        loads[n].wait()
        if n + AHEAD < len(loads):
            loads[n + AHEAD].start()
        for r in range(ROWS):
            at = 8 * r + 2 * s
            low = at_first * (pltpu.roll(first, 128 - at, 1) if at else first)
            high = at_last * pltpu.roll(last, 126 - at, 1)
            y_ref[n, r, :, :128] = y_ref[n, r, :, :128] + low
            y_ref[n, r, :, 128:] = y_ref[n, r, :, 128:] + high
        out_ref[n] = jnp.swapaxes(y_ref[n], 0, 1)
        stores[n].start()
    for store in stores:
        store.wait()


def order(y, edges):
    return pl.pallas_call(
        order_kernel,
        out_shape=jax.ShapeDtypeStruct((SAMPLES, HID, ROWS, COLS), BF16),
        in_specs=[HBM, VMEM],
        out_specs=HBM,
        scratch_shapes=[
            pltpu.VMEM((len(CHUNKS), ROWS, CHANNELS, COLS), BF16),
            pltpu.VMEM((len(CHUNKS), CHANNELS, ROWS, COLS), BF16),
            pltpu.SemaphoreType.DMA((len(CHUNKS),)),
            pltpu.SemaphoreType.DMA((len(CHUNKS),)),
        ],
        compiler_params=pltpu.CompilerParams(vmem_limit_bytes=LIMIT),
    )(y, edges)


def on_device(state, mask, fold, first_kernel, first_bias, second_kernel, second_bias):
    y, edges = main(state, mask, fold, jnp.transpose(first_kernel, (0, 2, 1)), first_bias[None], second_kernel, second_bias[None])
    return order(y, edges)


def solution(mesh):
    return jax.shard_map(
        on_device,
        mesh=mesh,
        in_specs=(P(None, None, "lat", "lon"), P(None, "lat", "lon"), P("lon"), P(), P(), P(), P()),
        out_specs=P(None, None, "lat", "lon"),
        check_vma=False,
    )
```

```python
import functools

import jax
import jax.numpy as jnp
from jax import lax
from jax.experimental import pallas as pl
from jax.experimental.pallas import tpu as pltpu
from jax.sharding import PartitionSpec as P

F32 = jnp.float32
BF16 = jnp.bfloat16
MESH = pl.DeviceIdType.MESH
VMEM = pl.BlockSpec(memory_space=pltpu.VMEM)
SMEM = pl.BlockSpec(memory_space=pltpu.SMEM)

SAMPLES, CIN, ROWS, COLS, HID = 4, 75, 8, 256, 256
CPAD = 80
WIDE = SAMPLES * COLS
XROWS = ROWS + 4
HROWS = ROWS + 2
NLON, NLAT = 16, 8
MAIN_LIMIT = 44 * 1024 * 1024
ORDER_LIMIT = 16 * 1024 * 1024


def lanes_of(shape):
    return lax.broadcasted_iota(jnp.int32, shape, len(shape) - 1)


def edge_pairs(x_ref, rows, pairs):
    pair = lax.shift_right_logical(lanes_of((CPAD, 128)), 1)
    pairs = list(pairs)
    for r in rows:
        for s in range(SAMPLES):
            row = x_ref[r, :, s * COLS : (s + 1) * COLS].astype(F32)
            at = 8 * r + 2 * s
            here = pair == at // 2
            for n, (half, by) in enumerate(((0, at), (0, at - 2), (1, at + 4), (1, at + 2))):
                part = pltpu.roll(row[:, half * 128 : half * 128 + 128], by % 128, 1)
                pairs[n] = jnp.where(here, part, pairs[n])
    return pairs


def prepare(state_ref, mask_ref, x_ref, t_ref):
    for s in range(SAMPLES):
        for h in range(2):
            cut = slice(h * 128, (h + 1) * 128)
            t_ref[s, h, CIN * ROWS : (CIN + 1) * ROWS, :] = mask_ref[0, :, cut].astype(F32)
            t_ref[s, h, (CIN + 1) * ROWS : (CIN + 4) * ROWS, :] = jnp.ones((3 * ROWS, 128), F32)
            t_ref[s, h, (CIN + 4) * ROWS :, :] = jnp.zeros(((CPAD - CIN - 4) * ROWS, 128), F32)
            masked = state_ref[s, :, :, cut].astype(F32) * mask_ref[:, :, cut].astype(F32)
            t_ref[s, h, : CIN * ROWS, :] = masked.reshape(CIN * ROWS, 128)
            for r in range(ROWS):
                at = s * COLS + h * 128
                x_ref[r + 2, :, at : at + 128] = t_ref[s, h, pl.ds(r, CPAD, stride=ROWS), :].astype(BF16)


def piece(i):
    return i // 8, (i // 2) % 4, i % 2


HALF = ((0, 48), (48, 32))


def gelu_times(x, half_surface):
    half = x * half_surface
    return half + half * jnp.tanh(x * (0.7978845608028654 + 0.035677408136300125 * (x * x)))


def wide_bias(ref):
    return jnp.transpose(jnp.broadcast_to(ref[...], (128, HID)))


def stack_taps(raw_ref, bias_ref, pad_ref, k1_ref, turned):
    pad_ref[9 * CPAD :, :] = jnp.zeros((pad_ref.shape[0] - 9 * CPAD, HID), F32)
    for t in range(9):
        at = CPAD * (8 - t if turned else t)
        pad_ref[at + 72 : at + CPAD, :] = jnp.zeros((8, HID), F32)
        pad_ref[at : at + CIN, :] = raw_ref[t].astype(F32)
    at = 4 * CPAD + CIN + 1
    rest = bias_ref[...]
    for n in range(3):
        part = rest.astype(BF16).astype(F32)
        pad_ref[at + n : at + n + 1, :] = part
        rest = rest - part
    k1_ref[1 if turned else 0] = jnp.transpose(pad_ref[...])[:, : 9 * CPAD].astype(BF16)


def shift_row(x_ref, xb_ref, r):
    row = x_ref[r]
    xb_ref[r, :CPAD, :] = pltpu.roll(row, 1, 1)
    xb_ref[r, CPAD : 2 * CPAD, :] = row
    xb_ref[r, 2 * CPAD :, :] = pltpu.roll(row, WIDE - 1, 1)


def hidden_row(x_ref, xb_ref, hb_ref, k1_ref, which, r):
    kernel = k1_ref[which]
    taps = xb_ref[r : r + 3].reshape(9 * CPAD, WIDE)
    for pair in range(2):
        cut = slice(pair * 2 * COLS, (pair + 1) * 2 * COLS)
        out = jnp.dot(kernel, taps[:, cut], preferred_element_type=F32)
        surface = x_ref[r + 1, 64:CPAD, cut].astype(F32)[CIN - 64 : CIN - 63]
        out = gelu_times(out, 0.5 * surface).astype(BF16)
        hb_ref[r, :HID, cut] = pltpu.roll(out, 1, 1)
        hb_ref[r, HID : 2 * HID, cut] = out
        hb_ref[r, 2 * HID :, cut] = pltpu.roll(out, 2 * COLS - 1, 1)


def output_row(x_ref, hb_ref, k2_ref, y_ref, bias, r):
    kernel = jnp.concatenate([k2_ref[t] for t in range(9)], 1)
    taps = hb_ref[r : r + 3].reshape(9 * HID, WIDE)
    column = jnp.bitwise_and(lanes_of((1, 2 * COLS)), COLS - 1)
    inner = jnp.logical_and(column >= 2, column < COLS - 2)
    for pair in range(2):
        cut = slice(pair * 2 * COLS, (pair + 1) * 2 * COLS)
        out = jnp.dot(kernel, taps[:, cut], preferred_element_type=F32)
        surface = x_ref[r + 2, 64:CPAD, cut].astype(F32)[CIN - 64 : CIN - 63]
        surface = jnp.where(inner, surface, 0.0)
        out = ((out + jnp.concatenate([bias] * 4, 1)) * surface).astype(BF16)
        y_ref[r, 2 * pair] = out[:, :COLS]
        y_ref[r, 2 * pair + 1] = out[:, COLS:]


def edge_columns(columns, k1_ref, k2_ref, bias2, top):
    lane = lanes_of((HID, 128))
    back = [[c if not a else pltpu.roll(c, 128 - 8 * a, 1) for a in range(3)] for c in columns]
    taps = jnp.concatenate(
        [jnp.concatenate([back[i + b][a] for a in range(3) for b in range(3)], 0).astype(BF16) for i in range(4)], 1
    )
    plain = jnp.dot(k1_ref[0], taps, preferred_element_type=F32)
    turned = jnp.dot(k1_ref[1], taps, preferred_element_type=F32)
    ghost = lane >= jnp.where(top, 72, 128)
    hidden = []
    for i in range(4):
        cut = slice(i * 128, (i + 1) * 128)
        out = jnp.where(ghost, turned[:, cut], plain[:, cut])
        out = gelu_times(out, 0.5 * back[i + 1][1][CIN : CIN + 1, :])
        hidden.append([out if not a else pltpu.roll(out, 128 - 8 * a, 1) for a in range(3)])
    taps = jnp.concatenate(
        [jnp.concatenate([hidden[i + b][a] for a in range(3) for b in range(3)], 0).astype(BF16) for i in range(2)], 1
    )
    kernel = jnp.concatenate([k2_ref[t] for t in range(9)], 1)
    out = jnp.dot(kernel, taps, preferred_element_type=F32)
    first, second = ((out[:, i * 128 : i * 128 + 128] + bias2) * back[i + 2][2][CIN : CIN + 1, :] for i in range(2))
    even = jnp.bitwise_and(lane, 1) == 0
    return jnp.where(even, first, pltpu.roll(second, 1, 1)), jnp.where(even, pltpu.roll(first, 127, 1), second)


def fold_kernel_parts(a_ref, y0_ref, y1_ref, s_ref, se_ref, fold_ref, lon):
    start = fold_ref[0]
    turn = jnp.bitwise_and(start, COLS - 1)
    block = lax.shift_right_logical(start, 8)
    source = lax.broadcasted_iota(jnp.int32, (COLS, COLS), 0)
    lane = lax.broadcasted_iota(jnp.int32, (COLS, COLS), 1)
    pieces = a_ref[...].reshape(NLON * 48, COLS)
    for y_ref, target in ((y0_ref, turn), (y1_ref, turn + COLS)):
        choose = jnp.where(source + lane == target, 1.0, 0.0).astype(BF16)
        y_ref[...] = jnp.dot(pieces, choose, preferred_element_type=F32).astype(BF16).reshape(NLON, 48, COLS)
    for d in range(NLON):
        b = jnp.bitwise_and(block + lon - d, NLON - 1)
        s_ref[d] = y0_ref[b] + y1_ref[jnp.bitwise_and(b + NLON - 1, NLON - 1)]
    group = lax.shift_right_logical(lane, 4)
    step = jnp.where(group >= 8, group - 16, group)
    k = jnp.bitwise_and(lane, 15)
    column = jnp.where(k < 2, k - 2, k + COLS - 2)
    hit = jnp.logical_and(k < 4, source == turn - column - COLS * step)
    outer = jnp.dot(pieces, jnp.where(hit, 1.0, 0.0).astype(BF16), preferred_element_type=F32).reshape(NLON, 48, COLS)
    total = jnp.zeros((48, COLS), F32)
    for e in range(NLON):
        total = total + pltpu.roll(outer[e], jnp.bitwise_and(16 * (block + lon - e), COLS - 1), 1)
    total = jnp.concatenate([total, jnp.zeros((80, COLS), F32)], 0)
    se_ref[...] = jnp.transpose(total).astype(BF16).reshape(NLON, 16, 128)


def fold_edges(fe_ref):
    sent = jnp.transpose(fe_ref[...].reshape(NLON * 16, 128).astype(F32)).astype(BF16)
    f = lax.broadcasted_iota(jnp.int32, (256, 512), 0)
    lane = lax.broadcasted_iota(jnp.int32, (256, 512), 1)
    to_lane, side, half = jnp.bitwise_and(lane, 127), jnp.bitwise_and(lane // 128, 1), lane // 256
    hit = jnp.logical_and(
        jnp.bitwise_and(f // 16, 1) == half,
        jnp.logical_and(
            jnp.bitwise_and(f, 15) == 2 * side + jnp.bitwise_and(to_lane, 1),
            to_lane // 2 == 40 + (f // 128) * 4 + jnp.bitwise_and(f // 32, 3),
        ),
    )
    got = jnp.dot(sent, jnp.where(hit, 1.0, 0.0).astype(BF16), preferred_element_type=F32)
    return [jnp.concatenate([got[:48, n : n + 128], got[:32, 256 + n : 384 + n]], 0) for n in (0, 128)]


def main_kernel(
    state_hbm, mask_hbm, fold_ref, k1_hbm, b1_ref, k2_hbm, b2_ref, y_hbm, edge_out,
    state_ref, mask_ref, k1_raw, k1_pad, k1_ref, k2_ref, x_ref, t_ref, xb_ref, hb_ref, y_ref,
    sp_ref, lp_ref, rp_ref, relay_ref, a_ref, y0_ref, y1_ref, s_ref, se_ref, fe_ref, ft_ref,
    load_sem, store_sem,
    row_send, row_recv, relay_send, relay_recv, pass_send, pass_recv, edge_send, edge_recv, f1_send, f1_recv, f2_send, f2_recv, f3_send, f3_recv,
):
    loads = [
        pltpu.make_async_copy(src, dst, load_sem.at[n])
        for n, (src, dst) in enumerate(((mask_hbm, mask_ref), (state_hbm, state_ref), (k1_hbm, k1_raw), (k2_hbm, k2_ref)))
    ]
    for n in (2, 0, 1, 3):
        loads[n].start()
    lon = lax.axis_index("lon")
    lat = lax.axis_index("lat")
    right, left = lax.rem(lon + 1, NLON), lax.rem(lon + NLON - 1, NLON)
    top = lat == NLAT - 1
    has = {-1: lat > 0, 0: None, 1: lat < NLAT - 1}

    def when(flag, fn):
        if flag is None:
            fn()
        else:
            pl.when(flag)(fn)

    barrier = pltpu.get_barrier_semaphore()

    def greet(at_lat, at_lon):
        pl.semaphore_signal(barrier, inc=1, device_id={"lat": at_lat, "lon": at_lon}, device_id_type=MESH)

    for d in (-1, 0, 1):
        def hello(d=d):
            if d:
                greet(lat + d, lon)
            greet(lat + d, left)
            greet(lat + d, right)
        when(has[d], hello)

    @pl.when(top)
    def _():
        for k in range(2, NLON - 1):
            greet(lat, lax.rem(lon + k, NLON))

    is_relay, is_low, is_high = lat == 0, lat == NLAT // 2 - 1, lat == NLAT // 2
    pl.when(is_relay)(lambda: [greet(NLAT // 2 - 1, lon), greet(NLAT // 2, lon)] and None)
    pl.when(jnp.logical_or(is_low, is_high))(lambda: greet(0, lon))

    loads[2].wait()
    stack_taps(k1_raw, b1_ref, k1_pad, k1_ref, False)
    bias2 = wide_bias(b2_ref)
    loads[0].wait()
    loads[1].wait()
    prepare(state_ref, mask_ref, x_ref, t_ref)

    def hidden(r, which=0):
        hidden_row(x_ref, xb_ref, hb_ref, k1_ref, which, r)

    stores = []

    def output(r):
        output_row(x_ref, hb_ref, k2_ref, y_ref, bias2, r)
        stores.append(pltpu.make_async_copy(y_ref.at[r], y_hbm.at[:, r], store_sem.at[r]))
        stores[-1].start()

    @pl.when(lat == 0)
    def _():
        x_ref[0:2] = jnp.zeros((2, CPAD, WIDE), BF16)
        lp_ref[0:16] = jnp.zeros((16, 128), BF16)
        rp_ref[0:16] = jnp.zeros((16, 128), BF16)

    @pl.when(jnp.logical_or(is_low, is_high))
    def _():
        pl.semaphore_wait(barrier, 9)

    @pl.when(jnp.logical_and(jnp.logical_and(lat > 0, lat < NLAT - 1), jnp.logical_not(jnp.logical_or(is_low, is_high))))
    def _():
        pl.semaphore_wait(barrier, 8)

    @pl.when(lat == 0)
    def _():
        pl.semaphore_wait(barrier, 7)

    @pl.when(top)
    def _():
        pl.semaphore_wait(barrier, 18)

    def to(src, dst, send, recv, at_lat, at_lon):
        return pltpu.make_async_remote_copy(
            src_ref=src, dst_ref=dst, send_sem=send, recv_sem=recv,
            device_id={"lat": at_lat, "lon": at_lon}, device_id_type=MESH,
        )

    def first_copy(i):
        row, s, half = piece(i)
        at, n = HALF[half]
        return to(
            x_ref.at[9 - row, pl.ds(at, n), pl.ds(s * COLS, COLS)], a_ref.at[lon, pl.ds(0, n)],
            f1_send.at[i], f1_recv.at[lon], lat, i,
        )

    my_row, my_s, my_half = piece(lon)

    def second_copy(d, half):
        at, n = HALF[half]
        return to(
            s_ref.at[d, pl.ds(0, n)],
            x_ref.at[10 + my_row, pl.ds(at, n), pl.ds(pl.multiple_of(my_s * COLS, COLS), COLS)],
            f2_send.at[d], f2_recv.at[lon], lat, d,
        )

    def third_copy(d):
        return to(se_ref.at[d], fe_ref.at[lon], f3_send.at[d], f3_recv.at[lon], lat, d)

    up = to(x_ref.at[pl.ds(8, 2)], x_ref.at[pl.ds(0, 2)], row_send.at[0], row_recv.at[0], lat + 1, lon)
    def relay_copy(s):
        return to(
            x_ref.at[pl.ds(2, 2), :, pl.ds(s * COLS, COLS)], relay_ref.at[s],
            relay_send.at[s], relay_recv.at[s], 0, lon,
        )

    def pass_copy(s):
        return to(
            relay_ref.at[s], x_ref.at[pl.ds(10, 2), :, pl.ds(s * COLS, COLS)],
            pass_send.at[s], pass_recv.at[s], NLAT // 2 - 1, lon,
        )

    def hand_on(s):
        @pl.when(is_relay)
        def _():
            relay_copy(s).wait_recv()
            pass_copy(s).start()

    direct = jnp.logical_and(lat > 0, jnp.logical_not(is_high))
    down = to(x_ref.at[pl.ds(2, 2)], x_ref.at[pl.ds(10, 2)], row_send.at[1], row_recv.at[1], lat - 1, lon)
    edge = {}
    for d, at, n, there in ((-1, 16, 16, 80), (0, 16, 64, 16), (1, 64, 16, 0)):
        edge[d] = (
            to(sp_ref.at[0, pl.ds(at, n)], rp_ref.at[pl.ds(there, n)], edge_send.at[d + 1], edge_recv.at[1 - d], lat + d, left),
            to(sp_ref.at[1, pl.ds(at, n)], lp_ref.at[pl.ds(there, n)], edge_send.at[d + 4], edge_recv.at[4 - d], lat + d, right),
        )

    @pl.when(top)
    def _():
        for i in range(NLON):
            pl.when(i != lon)(lambda i=i: first_copy(i).start())

    @pl.when(is_high)
    def _():
        for s in range(SAMPLES):
            relay_copy(s).start()

    pl.when(has[1])(lambda: up.start())
    pl.when(direct)(lambda: down.start())
    pairs = edge_pairs(x_ref, range(2, 2 + ROWS), [jnp.zeros((CPAD, 128), F32)] * 4)
    for n, pair in enumerate((pairs[0], pairs[3])):
        sp_ref[n] = jnp.transpose(jnp.concatenate([pair, jnp.zeros((48, 128), F32)], 0)).astype(BF16)
    for d in (-1, 0, 1):
        def go(d=d):
            edge[d][0].start()
            edge[d][1].start()
        when(has[d], go)
    for r in range(2, 2 + ROWS):
        shift_row(x_ref, xb_ref, r)

    for r in range(2, HROWS - 2):
        hidden(r)
    loads[3].wait()
    output(2)

    @pl.when(top)
    def _():
        for half in (0, 1):
            at, n = HALF[half]

            @pl.when(my_half == half)
            def _():
                mine = x_ref.at[9 - my_row, pl.ds(at, n), pl.ds(pl.multiple_of(my_s * COLS, COLS), COLS)]
                a_ref[lon, 0:n] = mine[...]
                if n < 48:
                    a_ref[:, n:] = jnp.zeros((NLON, 48 - n, COLS), BF16)
                for e in range(NLON):
                    def arrive(e=e):
                        to(a_ref.at[e, pl.ds(0, n)], a_ref.at[e, pl.ds(0, n)], f1_send.at[e], f1_recv.at[e], lat, e).wait_recv()
                    pl.when(e != lon)(arrive)

        fold_kernel_parts(a_ref, y0_ref, y1_ref, s_ref, se_ref, fold_ref, lon)
        for half in (0, 1):
            at, n = HALF[half]

            @pl.when(my_half == half)
            def _():
                for d in range(NLON):
                    pl.when(d != lon)(lambda d=d: second_copy(d, half).start())
                x_ref[10 + my_row, at : at + n, pl.ds(pl.multiple_of(my_s * COLS, COLS), COLS)] = s_ref[lon, 0:n]
        for d in range(NLON):
            pl.when(d != lon)(lambda d=d: third_copy(d).start())
        fe_ref[lon] = se_ref[lon]

    hand_on(0)
    output(3)
    hand_on(1)
    output(4)
    hand_on(2)
    output(5)

    @pl.when(top)
    def _():
        stack_taps(k1_raw, b1_ref, k1_pad, k1_ref, True)

    pl.when(has[-1])(lambda: up.wait_recv())
    shift_row(x_ref, xb_ref, 0)
    shift_row(x_ref, xb_ref, 1)
    hand_on(3)
    hidden(1)
    hidden(0)
    output(1)
    output(0)

    pl.when(jnp.logical_and(has[1], jnp.logical_not(is_low)))(lambda: down.wait_recv())

    @pl.when(is_low)
    def _():
        for s in range(SAMPLES):
            pass_copy(s).wait_recv()

    @pl.when(top)
    def _():
        for e in range(NLON):
            row, s, half = piece(e)
            at, n = HALF[half]
            def arrive(e=e, row=row, s=s, at=at, n=n):
                there = x_ref.at[10 + row, pl.ds(at, n), pl.ds(s * COLS, COLS)]
                to(there, there, f2_send.at[e], f2_recv.at[e], lat, e).wait_recv()
                to(fe_ref.at[e], fe_ref.at[e], f3_send.at[e], f3_recv.at[e], lat, e).wait_recv()
            pl.when(e != lon)(arrive)
        for n, part in enumerate(fold_edges(fe_ref)):
            ft_ref[n] = part

    shift_row(x_ref, xb_ref, ROWS + 2)
    shift_row(x_ref, xb_ref, ROWS + 3)
    hidden(ROWS)
    hidden(ROWS + 1, jnp.where(top, 1, 0))
    output(6)
    output(7)

    for d in (-1, 0, 1):
        def got(d=d):
            edge[-d][0].wait_recv()
            edge[-d][1].wait_recv()
        when(has[d], got)
    pairs = edge_pairs(x_ref, (0, 1, 10, 11), pairs)
    lane = lanes_of((CPAD, 128))

    def joined(ref, n):
        sent = jnp.transpose(ref[...].astype(F32))[:CPAD]
        return jnp.where(jnp.logical_and(top, lane >= 80), ft_ref[n], sent)

    before, after = joined(lp_ref, 0), joined(rp_ref, 1)
    even = jnp.bitwise_and(lane, 1) == 0
    columns = []
    for low, high in ((before, pairs[2]), (pairs[0], pairs[3]), (pairs[1], after)):
        columns.append(jnp.where(even, low, pltpu.roll(high, 1, 1)))
        columns.append(jnp.where(even, pltpu.roll(low, 127, 1), high))
    first, last = edge_columns(columns, k1_ref, k2_ref, bias2, top)
    used = lanes_of((HID, 128)) < 64
    edge_out[0] = jnp.where(used, first, 0.0).astype(BF16)
    edge_out[1] = jnp.where(used, last, 0.0).astype(BF16)

    pl.when(has[1])(lambda: up.wait_send())
    pl.when(direct)(lambda: down.wait_send())

    @pl.when(is_high)
    def _():
        for s in range(SAMPLES):
            relay_copy(s).wait_send()

    @pl.when(is_relay)
    def _():
        for s in range(SAMPLES):
            pass_copy(s).wait_send()

    for d in (-1, 0, 1):
        def sent(d=d):
            edge[d][0].wait_send()
            edge[d][1].wait_send()
        when(has[d], sent)

    @pl.when(top)
    def _():
        for i in range(NLON):
            pl.when(i != lon)(lambda i=i: first_copy(i).wait_send())
        for half in (0, 1):
            @pl.when(my_half == half)
            def _():
                for d in range(NLON):
                    pl.when(d != lon)(lambda d=d: second_copy(d, half).wait_send())
        for d in range(NLON):
            pl.when(d != lon)(lambda d=d: third_copy(d).wait_send())
    for store in stores:
        store.wait()


HBM = pl.BlockSpec(memory_space=pl.ANY)


def main(state, mask, fold, k1, b1, k2, b2):
    dma = pltpu.SemaphoreType.DMA
    return pl.pallas_call(
        main_kernel,
        out_shape=(
            jax.ShapeDtypeStruct((SAMPLES, ROWS, HID, COLS), BF16),
            jax.ShapeDtypeStruct((2, HID, 128), BF16),
        ),
        in_specs=[HBM, HBM, SMEM, HBM, VMEM, HBM, VMEM],
        out_specs=(HBM, VMEM),
        scratch_shapes=[
            pltpu.VMEM(state.shape, BF16),
            pltpu.VMEM(mask.shape, jnp.int32),
            pltpu.VMEM(k1.shape, BF16),
            pltpu.VMEM((6 * 128, HID), F32),
            pltpu.VMEM((2, HID, 9 * CPAD), BF16),
            pltpu.VMEM(k2.shape, BF16),
            pltpu.VMEM((XROWS, CPAD, WIDE), BF16),
            pltpu.VMEM((SAMPLES, 2, CPAD * ROWS, 128), F32),
            pltpu.VMEM((XROWS, 3 * CPAD, WIDE), BF16),
            pltpu.VMEM((HROWS, 3 * HID, WIDE), BF16),
            pltpu.VMEM((ROWS, SAMPLES, HID, COLS), BF16),
            pltpu.VMEM((2, 128, 128), BF16),
            pltpu.VMEM((128, 128), BF16),
            pltpu.VMEM((128, 128), BF16),
            pltpu.VMEM((SAMPLES, 2, CPAD, COLS), BF16),
            pltpu.VMEM((NLON, 48, COLS), BF16),
            pltpu.VMEM((NLON, 48, COLS), BF16),
            pltpu.VMEM((NLON, 48, COLS), BF16),
            pltpu.VMEM((NLON, 48, COLS), BF16),
            pltpu.VMEM((NLON, 16, 128), BF16),
            pltpu.VMEM((NLON, 16, 128), BF16),
            pltpu.VMEM((2, CPAD, 128), F32),
            dma((4,)), dma((ROWS,)),
            dma((2,)), dma((2,)), dma((SAMPLES,)), dma((SAMPLES,)), dma((SAMPLES,)), dma((SAMPLES,)), dma((6,)), dma((6,)),
            dma((NLON,)), dma((NLON,)), dma((NLON,)), dma((NLON,)), dma((NLON,)), dma((NLON,)),
        ],
        compiler_params=pltpu.CompilerParams(collective_id=0, has_side_effects=True, vmem_limit_bytes=MAIN_LIMIT),
    )(state, mask, fold, k1, b1, k2, b2)


CHANNELS = 128
AHEAD = 8
CHUNKS = [(s, c) for s in range(SAMPLES) for c in range(HID // CHANNELS)]


def order_kernel(y_hbm, edge_ref, out_hbm, y_ref, out_ref, load_sem, store_sem):
    loads, stores = [], []
    for n, (s, c) in enumerate(CHUNKS):
        part = pl.ds(c * CHANNELS, CHANNELS)
        loads.append(pltpu.make_async_copy(y_hbm.at[s, :, part], y_ref.at[n], load_sem.at[n]))
        stores.append(pltpu.make_async_copy(out_ref.at[n], out_hbm.at[s, part], store_sem.at[n]))
    for load in loads[:AHEAD]:
        load.start()
    lane = lanes_of((CHANNELS, 128))
    at_first = jnp.where(lane < 2, 1.0, 0.0).astype(BF16)
    at_last = jnp.where(lane >= 126, 1.0, 0.0).astype(BF16)
    for n, (s, c) in enumerate(CHUNKS):
        cut = slice(c * CHANNELS, (c + 1) * CHANNELS)
        first, last = edge_ref[0, cut], edge_ref[1, cut]
        loads[n].wait()
        if n + AHEAD < len(loads):
            loads[n + AHEAD].start()
        for r in range(ROWS):
            at = 8 * r + 2 * s
            low = at_first * (pltpu.roll(first, 128 - at, 1) if at else first)
            high = at_last * pltpu.roll(last, 126 - at, 1)
            y_ref[n, r, :, :128] = y_ref[n, r, :, :128] + low
            y_ref[n, r, :, 128:] = y_ref[n, r, :, 128:] + high
        out_ref[n] = jnp.swapaxes(y_ref[n], 0, 1)
        stores[n].start()
    for store in stores:
        store.wait()


def order(y, edges):
    return pl.pallas_call(
        order_kernel,
        out_shape=jax.ShapeDtypeStruct((SAMPLES, HID, ROWS, COLS), BF16),
        in_specs=[HBM, VMEM],
        out_specs=HBM,
        scratch_shapes=[
            pltpu.VMEM((len(CHUNKS), ROWS, CHANNELS, COLS), BF16),
            pltpu.VMEM((len(CHUNKS), CHANNELS, ROWS, COLS), BF16),
            pltpu.SemaphoreType.DMA((len(CHUNKS),)),
            pltpu.SemaphoreType.DMA((len(CHUNKS),)),
        ],
        compiler_params=pltpu.CompilerParams(vmem_limit_bytes=ORDER_LIMIT),
    )(y, edges)


def on_device(state, mask, fold, first_kernel, first_bias, second_kernel, second_bias):
    y, edges = main(state, mask, fold, jnp.transpose(first_kernel, (0, 2, 1)), first_bias[None], second_kernel, second_bias[None])
    return order(y, edges)


def solution(mesh):
    return jax.shard_map(
        on_device,
        mesh=mesh,
        in_specs=(P(None, None, "lat", "lon"), P(None, "lat", "lon"), P("lon"), P(), P(), P(), P()),
        out_specs=P(None, None, "lat", "lon"),
        check_vma=False,
    )
```

```python
import functools

import jax
import jax.numpy as jnp
from jax import lax
from jax.experimental import pallas as pl
from jax.experimental.pallas import tpu as pltpu
from jax.sharding import PartitionSpec as P

F32 = jnp.float32
BF16 = jnp.bfloat16
MESH = pl.DeviceIdType.MESH
VMEM = pl.BlockSpec(memory_space=pltpu.VMEM)
SMEM = pl.BlockSpec(memory_space=pltpu.SMEM)

SAMPLES, CIN, ROWS, COLS, HID = 4, 75, 8, 256, 256
CPAD = 80
WIDE = SAMPLES * COLS
XROWS = ROWS + 4
HROWS = ROWS + 2
NLON, NLAT = 16, 8
LIMIT = 60 * 1024 * 1024


def lanes_of(shape):
    return lax.broadcasted_iota(jnp.int32, shape, len(shape) - 1)


def edge_pairs(x_ref, rows, pairs):
    pair = lax.shift_right_logical(lanes_of((CPAD, 128)), 1)
    pairs = list(pairs)
    for r in rows:
        for s in range(SAMPLES):
            row = x_ref[r, :, s * COLS : (s + 1) * COLS].astype(F32)
            at = 8 * r + 2 * s
            here = pair == at // 2
            for n, (half, by) in enumerate(((0, at), (0, at - 2), (1, at + 4), (1, at + 2))):
                part = pltpu.roll(row[:, half * 128 : half * 128 + 128], by % 128, 1)
                pairs[n] = jnp.where(here, part, pairs[n])
    return pairs


def prepare(state_ref, mask_ref, x_ref, t_ref, s):
    for h in range(2):
        cut = slice(h * 128, (h + 1) * 128)
        t_ref[s, h, CIN * ROWS : (CIN + 1) * ROWS, :] = mask_ref[0, :, cut].astype(F32)
        t_ref[s, h, (CIN + 1) * ROWS : (CIN + 4) * ROWS, :] = jnp.ones((3 * ROWS, 128), F32)
        t_ref[s, h, (CIN + 4) * ROWS :, :] = jnp.zeros(((CPAD - CIN - 4) * ROWS, 128), F32)
        masked = state_ref[s, :, :, cut].astype(F32) * mask_ref[:, :, cut].astype(F32)
        t_ref[s, h, : CIN * ROWS, :] = masked.reshape(CIN * ROWS, 128)
        for r in range(ROWS):
            at = s * COLS + h * 128
            x_ref[r + 2, :, at : at + 128] = t_ref[s, h, pl.ds(r, CPAD, stride=ROWS), :].astype(BF16)


def piece(i):
    return i // 8, (i // 2) % 4, i % 2


HALF = ((0, 48), (48, 32))


def gelu_times(x, half_surface):
    half = x * half_surface
    return half + half * jnp.tanh(x * (0.7978845608028654 + 0.035677408136300125 * (x * x)))


def wide_bias(ref):
    return jnp.transpose(jnp.broadcast_to(ref[...], (128, HID)))


def stack_taps(raw_ref, bias_ref, pad_ref, k1_ref, turned):
    pad_ref[9 * CPAD :, :] = jnp.zeros((pad_ref.shape[0] - 9 * CPAD, HID), F32)
    for t in range(9):
        at = CPAD * (8 - t if turned else t)
        pad_ref[at + 72 : at + CPAD, :] = jnp.zeros((8, HID), F32)
        pad_ref[at : at + CIN, :] = raw_ref[t].astype(F32)
    at = 4 * CPAD + CIN + 1
    rest = bias_ref[...]
    for n in range(3):
        part = rest.astype(BF16).astype(F32)
        pad_ref[at + n : at + n + 1, :] = part
        rest = rest - part
    k1_ref[1 if turned else 0] = jnp.transpose(pad_ref[...])[:, : 9 * CPAD].astype(BF16)


def shift_row(x_ref, xb_ref, r):
    row = x_ref[r]
    xb_ref[r, :CPAD, :] = pltpu.roll(row, 1, 1)
    xb_ref[r, CPAD : 2 * CPAD, :] = row
    xb_ref[r, 2 * CPAD :, :] = pltpu.roll(row, WIDE - 1, 1)


def hidden_row(x_ref, xb_ref, hb_ref, k1_ref, which, r):
    kernel = k1_ref[which]
    taps = xb_ref[r : r + 3].reshape(9 * CPAD, WIDE)
    for pair in range(2):
        cut = slice(pair * 2 * COLS, (pair + 1) * 2 * COLS)
        out = jnp.dot(kernel, taps[:, cut], preferred_element_type=F32)
        surface = x_ref[r + 1, 64:CPAD, cut].astype(F32)[CIN - 64 : CIN - 63]
        out = gelu_times(out, 0.5 * surface).astype(BF16)
        hb_ref[r, :HID, cut] = pltpu.roll(out, 1, 1)
        hb_ref[r, HID : 2 * HID, cut] = out
        hb_ref[r, 2 * HID :, cut] = pltpu.roll(out, 2 * COLS - 1, 1)


def output_row(x_ref, hb_ref, k2_ref, y_ref, bias, r):
    kernel = jnp.concatenate([k2_ref[t] for t in range(9)], 1)
    taps = hb_ref[r : r + 3].reshape(9 * HID, WIDE)
    column = jnp.bitwise_and(lanes_of((1, 2 * COLS)), COLS - 1)
    inner = jnp.logical_and(column >= 2, column < COLS - 2)
    for pair in range(2):
        cut = slice(pair * 2 * COLS, (pair + 1) * 2 * COLS)
        out = jnp.dot(kernel, taps[:, cut], preferred_element_type=F32)
        surface = x_ref[r + 2, 64:CPAD, cut].astype(F32)[CIN - 64 : CIN - 63]
        surface = jnp.where(inner, surface, 0.0)
        out = ((out + jnp.concatenate([bias] * 4, 1)) * surface).astype(BF16)
        y_ref[r, 2 * pair] = out[:, :COLS]
        y_ref[r, 2 * pair + 1] = out[:, COLS:]


def edge_columns(columns, k1_ref, k2_ref, bias2, top):
    lane = lanes_of((HID, 128))
    back = [[c if not a else pltpu.roll(c, 128 - 8 * a, 1) for a in range(3)] for c in columns]
    taps = jnp.concatenate(
        [jnp.concatenate([back[i + b][a] for a in range(3) for b in range(3)], 0).astype(BF16) for i in range(4)], 1
    )
    plain = jnp.dot(k1_ref[0], taps, preferred_element_type=F32)
    turned = jnp.dot(k1_ref[1], taps, preferred_element_type=F32)
    ghost = lane >= jnp.where(top, 72, 128)
    hidden = []
    for i in range(4):
        cut = slice(i * 128, (i + 1) * 128)
        out = jnp.where(ghost, turned[:, cut], plain[:, cut])
        out = gelu_times(out, 0.5 * back[i + 1][1][CIN : CIN + 1, :])
        hidden.append([out if not a else pltpu.roll(out, 128 - 8 * a, 1) for a in range(3)])
    taps = jnp.concatenate(
        [jnp.concatenate([hidden[i + b][a] for a in range(3) for b in range(3)], 0).astype(BF16) for i in range(2)], 1
    )
    kernel = jnp.concatenate([k2_ref[t] for t in range(9)], 1)
    out = jnp.dot(kernel, taps, preferred_element_type=F32)
    first, second = ((out[:, i * 128 : i * 128 + 128] + bias2) * back[i + 2][2][CIN : CIN + 1, :] for i in range(2))
    even = jnp.bitwise_and(lane, 1) == 0
    return jnp.where(even, first, pltpu.roll(second, 1, 1)), jnp.where(even, pltpu.roll(first, 127, 1), second)


def fold_kernel_parts(a_ref, y0_ref, y1_ref, s_ref, se_ref, fold_ref, lon):
    start = fold_ref[0]
    turn = jnp.bitwise_and(start, COLS - 1)
    block = lax.shift_right_logical(start, 8)
    source = lax.broadcasted_iota(jnp.int32, (COLS, COLS), 0)
    lane = lax.broadcasted_iota(jnp.int32, (COLS, COLS), 1)
    pieces = a_ref[...].reshape(NLON * 48, COLS)
    for y_ref, target in ((y0_ref, turn), (y1_ref, turn + COLS)):
        choose = jnp.where(source + lane == target, 1.0, 0.0).astype(BF16)
        y_ref[...] = jnp.dot(pieces, choose, preferred_element_type=F32).astype(BF16).reshape(NLON, 48, COLS)
    for d in range(NLON):
        b = jnp.bitwise_and(block + lon - d, NLON - 1)
        s_ref[d] = y0_ref[b] + y1_ref[jnp.bitwise_and(b + NLON - 1, NLON - 1)]
    group = lax.shift_right_logical(lane, 4)
    step = jnp.where(group >= 8, group - 16, group)
    k = jnp.bitwise_and(lane, 15)
    column = jnp.where(k < 2, k - 2, k + COLS - 2)
    hit = jnp.logical_and(k < 4, source == turn - column - COLS * step)
    outer = jnp.dot(pieces, jnp.where(hit, 1.0, 0.0).astype(BF16), preferred_element_type=F32).reshape(NLON, 48, COLS)
    total = jnp.zeros((48, COLS), F32)
    for e in range(NLON):
        total = total + pltpu.roll(outer[e], jnp.bitwise_and(16 * (block + lon - e), COLS - 1), 1)
    total = jnp.concatenate([total, jnp.zeros((80, COLS), F32)], 0)
    se_ref[...] = jnp.transpose(total).astype(BF16).reshape(NLON, 16, 128)


def fold_edges(fe_ref):
    sent = jnp.transpose(fe_ref[...].reshape(NLON * 16, 128).astype(F32)).astype(BF16)
    f = lax.broadcasted_iota(jnp.int32, (256, 512), 0)
    lane = lax.broadcasted_iota(jnp.int32, (256, 512), 1)
    to_lane, side, half = jnp.bitwise_and(lane, 127), jnp.bitwise_and(lane // 128, 1), lane // 256
    hit = jnp.logical_and(
        jnp.bitwise_and(f // 16, 1) == half,
        jnp.logical_and(
            jnp.bitwise_and(f, 15) == 2 * side + jnp.bitwise_and(to_lane, 1),
            to_lane // 2 == 40 + (f // 128) * 4 + jnp.bitwise_and(f // 32, 3),
        ),
    )
    got = jnp.dot(sent, jnp.where(hit, 1.0, 0.0).astype(BF16), preferred_element_type=F32)
    return [jnp.concatenate([got[:48, n : n + 128], got[:32, 256 + n : 384 + n]], 0) for n in (0, 128)]


def main_kernel(
    state_hbm, mask_hbm, fold_ref, k1_hbm, b1_ref, k2_hbm, b2_ref, y_hbm, edge_out,
    state_ref, mask_ref, k1_raw, k1_pad, k1_ref, k2_ref, x_ref, t_ref, xb_ref, hb_ref, y_ref,
    sp_ref, lp_ref, rp_ref, relay_ref, a_ref, y0_ref, y1_ref, s_ref, se_ref, fe_ref, ft_ref,
    load_sem, store_sem,
    row_send, row_recv, relay_send, relay_recv, pass_send, pass_recv, edge_send, edge_recv, f1_send, f1_recv, f2_send, f2_recv, f3_send, f3_recv,
):
    loads = [
        pltpu.make_async_copy(src, dst, load_sem.at[n])
        for n, (src, dst) in enumerate(
            [(mask_hbm, mask_ref), (k1_hbm, k1_raw), (k2_hbm, k2_ref)]
            + [(state_hbm.at[s], state_ref.at[s]) for s in range(SAMPLES)]
        )
    ]
    for n in (1, 0, 3, 4, 5, 6, 2):
        loads[n].start()
    lon = lax.axis_index("lon")
    lat = lax.axis_index("lat")
    right, left = lax.rem(lon + 1, NLON), lax.rem(lon + NLON - 1, NLON)
    top = lat == NLAT - 1
    has = {-1: lat > 0, 0: None, 1: lat < NLAT - 1}

    def when(flag, fn):
        if flag is None:
            fn()
        else:
            pl.when(flag)(fn)

    barrier = pltpu.get_barrier_semaphore()

    def greet(at_lat, at_lon):
        pl.semaphore_signal(barrier, inc=1, device_id={"lat": at_lat, "lon": at_lon}, device_id_type=MESH)

    for d in (-1, 0, 1):
        def hello(d=d):
            if d:
                greet(lat + d, lon)
            greet(lat + d, left)
            greet(lat + d, right)
        when(has[d], hello)

    @pl.when(top)
    def _():
        for k in range(2, NLON - 1):
            greet(lat, lax.rem(lon + k, NLON))

    is_relay, is_low, is_high = lat == 0, lat == NLAT // 2 - 1, lat == NLAT // 2
    pl.when(is_relay)(lambda: [greet(NLAT // 2 - 1, lon), greet(NLAT // 2, lon)] and None)
    pl.when(jnp.logical_or(is_low, is_high))(lambda: greet(0, lon))

    loads[1].wait()
    stack_taps(k1_raw, b1_ref, k1_pad, k1_ref, False)
    bias2 = wide_bias(b2_ref)
    loads[0].wait()
    for s in range(SAMPLES):
        loads[3 + s].wait()
        prepare(state_ref, mask_ref, x_ref, t_ref, s)

    def hidden(r, which=0):
        hidden_row(x_ref, xb_ref, hb_ref, k1_ref, which, r)

    stores = []

    def output(r):
        output_row(x_ref, hb_ref, k2_ref, y_ref, bias2, r)
        stores.append(pltpu.make_async_copy(y_ref.at[r], y_hbm.at[:, r], store_sem.at[r]))
        stores[-1].start()

    @pl.when(lat == 0)
    def _():
        x_ref[0:2] = jnp.zeros((2, CPAD, WIDE), BF16)
        lp_ref[0:16] = jnp.zeros((16, 128), BF16)
        rp_ref[0:16] = jnp.zeros((16, 128), BF16)

    @pl.when(jnp.logical_or(is_low, is_high))
    def _():
        pl.semaphore_wait(barrier, 9)

    @pl.when(jnp.logical_and(jnp.logical_and(lat > 0, lat < NLAT - 1), jnp.logical_not(jnp.logical_or(is_low, is_high))))
    def _():
        pl.semaphore_wait(barrier, 8)

    @pl.when(lat == 0)
    def _():
        pl.semaphore_wait(barrier, 7)

    @pl.when(top)
    def _():
        pl.semaphore_wait(barrier, 18)

    def to(src, dst, send, recv, at_lat, at_lon):
        return pltpu.make_async_remote_copy(
            src_ref=src, dst_ref=dst, send_sem=send, recv_sem=recv,
            device_id={"lat": at_lat, "lon": at_lon}, device_id_type=MESH,
        )

    def first_copy(i):
        row, s, half = piece(i)
        at, n = HALF[half]
        return to(
            x_ref.at[9 - row, pl.ds(at, n), pl.ds(s * COLS, COLS)], a_ref.at[lon, pl.ds(0, n)],
            f1_send.at[i], f1_recv.at[lon], lat, i,
        )

    my_row, my_s, my_half = piece(lon)

    def second_copy(d, half):
        at, n = HALF[half]
        return to(
            s_ref.at[d, pl.ds(0, n)],
            x_ref.at[10 + my_row, pl.ds(at, n), pl.ds(pl.multiple_of(my_s * COLS, COLS), COLS)],
            f2_send.at[d], f2_recv.at[lon], lat, d,
        )

    def third_copy(d):
        return to(se_ref.at[d], fe_ref.at[lon], f3_send.at[d], f3_recv.at[lon], lat, d)

    up = to(x_ref.at[pl.ds(8, 2)], x_ref.at[pl.ds(0, 2)], row_send.at[0], row_recv.at[0], lat + 1, lon)
    def relay_copy(s):
        return to(
            x_ref.at[pl.ds(2, 2), :, pl.ds(s * COLS, COLS)], relay_ref.at[s],
            relay_send.at[s], relay_recv.at[s], 0, lon,
        )

    def pass_copy(s):
        return to(
            relay_ref.at[s], x_ref.at[pl.ds(10, 2), :, pl.ds(s * COLS, COLS)],
            pass_send.at[s], pass_recv.at[s], NLAT // 2 - 1, lon,
        )

    def hand_on(s):
        @pl.when(is_relay)
        def _():
            relay_copy(s).wait_recv()
            pass_copy(s).start()

    direct = jnp.logical_and(lat > 0, jnp.logical_not(is_high))
    down = to(x_ref.at[pl.ds(2, 2)], x_ref.at[pl.ds(10, 2)], row_send.at[1], row_recv.at[1], lat - 1, lon)
    edge = {}
    for d, at, n, there in ((-1, 16, 16, 80), (0, 16, 64, 16), (1, 64, 16, 0)):
        edge[d] = (
            to(sp_ref.at[0, pl.ds(at, n)], rp_ref.at[pl.ds(there, n)], edge_send.at[d + 1], edge_recv.at[1 - d], lat + d, left),
            to(sp_ref.at[1, pl.ds(at, n)], lp_ref.at[pl.ds(there, n)], edge_send.at[d + 4], edge_recv.at[4 - d], lat + d, right),
        )

    @pl.when(top)
    def _():
        for i in range(NLON):
            pl.when(i != lon)(lambda i=i: first_copy(i).start())

    @pl.when(is_high)
    def _():
        for s in range(SAMPLES):
            relay_copy(s).start()

    pl.when(has[1])(lambda: up.start())
    pl.when(direct)(lambda: down.start())
    for r in range(2, 2 + ROWS):
        shift_row(x_ref, xb_ref, r)

    pairs = edge_pairs(x_ref, range(2, 2 + ROWS), [jnp.zeros((CPAD, 128), F32)] * 4)
    for n, pair in enumerate((pairs[0], pairs[3])):
        sp_ref[n] = jnp.transpose(jnp.concatenate([pair, jnp.zeros((48, 128), F32)], 0)).astype(BF16)
    for r in range(2, HROWS - 2):
        hidden(r)
    for d in (-1, 0, 1):
        def go(d=d):
            edge[d][0].start()
            edge[d][1].start()
        when(has[d], go)
    loads[2].wait()
    output(2)

    @pl.when(top)
    def _():
        for half in (0, 1):
            at, n = HALF[half]

            @pl.when(my_half == half)
            def _():
                mine = x_ref.at[9 - my_row, pl.ds(at, n), pl.ds(pl.multiple_of(my_s * COLS, COLS), COLS)]
                a_ref[lon, 0:n] = mine[...]
                if n < 48:
                    a_ref[:, n:] = jnp.zeros((NLON, 48 - n, COLS), BF16)
                for e in range(NLON):
                    def arrive(e=e):
                        to(a_ref.at[e, pl.ds(0, n)], a_ref.at[e, pl.ds(0, n)], f1_send.at[e], f1_recv.at[e], lat, e).wait_recv()
                    pl.when(e != lon)(arrive)

        fold_kernel_parts(a_ref, y0_ref, y1_ref, s_ref, se_ref, fold_ref, lon)
        for half in (0, 1):
            at, n = HALF[half]

            @pl.when(my_half == half)
            def _():
                for d in range(NLON):
                    pl.when(d != lon)(lambda d=d: second_copy(d, half).start())
                x_ref[10 + my_row, at : at + n, pl.ds(pl.multiple_of(my_s * COLS, COLS), COLS)] = s_ref[lon, 0:n]
        for d in range(NLON):
            pl.when(d != lon)(lambda d=d: third_copy(d).start())
        fe_ref[lon] = se_ref[lon]

    hand_on(0)
    output(3)
    hand_on(1)
    output(4)
    hand_on(2)
    output(5)

    @pl.when(top)
    def _():
        stack_taps(k1_raw, b1_ref, k1_pad, k1_ref, True)

    pl.when(has[-1])(lambda: up.wait_recv())
    shift_row(x_ref, xb_ref, 0)
    shift_row(x_ref, xb_ref, 1)
    hand_on(3)
    hidden(1)
    hidden(0)
    output(1)
    output(0)

    for d in (-1, 0, 1):
        def got(d=d):
            edge[-d][0].wait_recv()
            edge[-d][1].wait_recv()
        when(has[d], got)

    pl.when(jnp.logical_and(has[1], jnp.logical_not(is_low)))(lambda: down.wait_recv())

    @pl.when(is_low)
    def _():
        for s in range(SAMPLES):
            pass_copy(s).wait_recv()

    @pl.when(top)
    def _():
        for e in range(NLON):
            row, s, half = piece(e)
            at, n = HALF[half]
            def arrive(e=e, row=row, s=s, at=at, n=n):
                there = x_ref.at[10 + row, pl.ds(at, n), pl.ds(s * COLS, COLS)]
                to(there, there, f2_send.at[e], f2_recv.at[e], lat, e).wait_recv()
                to(fe_ref.at[e], fe_ref.at[e], f3_send.at[e], f3_recv.at[e], lat, e).wait_recv()
            pl.when(e != lon)(arrive)
        for n, part in enumerate(fold_edges(fe_ref)):
            ft_ref[n] = part

    shift_row(x_ref, xb_ref, ROWS + 2)
    shift_row(x_ref, xb_ref, ROWS + 3)
    hidden(ROWS)
    hidden(ROWS + 1, jnp.where(top, 1, 0))
    output(6)
    output(7)
    pairs = edge_pairs(x_ref, (0, 1, 10, 11), pairs)
    lane = lanes_of((CPAD, 128))

    def joined(ref, n):
        sent = jnp.transpose(ref[...].astype(F32))[:CPAD]
        return jnp.where(jnp.logical_and(top, lane >= 80), ft_ref[n], sent)

    before, after = joined(lp_ref, 0), joined(rp_ref, 1)
    even = jnp.bitwise_and(lane, 1) == 0
    columns = []
    for low, high in ((before, pairs[2]), (pairs[0], pairs[3]), (pairs[1], after)):
        columns.append(jnp.where(even, low, pltpu.roll(high, 1, 1)))
        columns.append(jnp.where(even, pltpu.roll(low, 127, 1), high))
    first, last = edge_columns(columns, k1_ref, k2_ref, bias2, top)
    used = lanes_of((HID, 128)) < 64
    edge_out[0] = jnp.where(used, first, 0.0).astype(BF16)
    edge_out[1] = jnp.where(used, last, 0.0).astype(BF16)

    pl.when(has[1])(lambda: up.wait_send())
    pl.when(direct)(lambda: down.wait_send())

    @pl.when(is_high)
    def _():
        for s in range(SAMPLES):
            relay_copy(s).wait_send()

    @pl.when(is_relay)
    def _():
        for s in range(SAMPLES):
            pass_copy(s).wait_send()

    for d in (-1, 0, 1):
        def sent(d=d):
            edge[d][0].wait_send()
            edge[d][1].wait_send()
        when(has[d], sent)

    @pl.when(top)
    def _():
        for i in range(NLON):
            pl.when(i != lon)(lambda i=i: first_copy(i).wait_send())
        for half in (0, 1):
            @pl.when(my_half == half)
            def _():
                for d in range(NLON):
                    pl.when(d != lon)(lambda d=d: second_copy(d, half).wait_send())
        for d in range(NLON):
            pl.when(d != lon)(lambda d=d: third_copy(d).wait_send())
    for store in stores:
        store.wait()


HBM = pl.BlockSpec(memory_space=pl.ANY)


def main(state, mask, fold, k1, b1, k2, b2):
    dma = pltpu.SemaphoreType.DMA
    return pl.pallas_call(
        main_kernel,
        out_shape=(
            jax.ShapeDtypeStruct((SAMPLES, ROWS, HID, COLS), BF16),
            jax.ShapeDtypeStruct((2, HID, 128), BF16),
        ),
        in_specs=[HBM, HBM, SMEM, HBM, VMEM, HBM, VMEM],
        out_specs=(HBM, VMEM),
        scratch_shapes=[
            pltpu.VMEM(state.shape, BF16),
            pltpu.VMEM(mask.shape, jnp.int32),
            pltpu.VMEM(k1.shape, BF16),
            pltpu.VMEM((6 * 128, HID), F32),
            pltpu.VMEM((2, HID, 9 * CPAD), BF16),
            pltpu.VMEM(k2.shape, BF16),
            pltpu.VMEM((XROWS, CPAD, WIDE), BF16),
            pltpu.VMEM((SAMPLES, 2, CPAD * ROWS, 128), F32),
            pltpu.VMEM((XROWS, 3 * CPAD, WIDE), BF16),
            pltpu.VMEM((HROWS, 3 * HID, WIDE), BF16),
            pltpu.VMEM((ROWS, SAMPLES, HID, COLS), BF16),
            pltpu.VMEM((2, 128, 128), BF16),
            pltpu.VMEM((128, 128), BF16),
            pltpu.VMEM((128, 128), BF16),
            pltpu.VMEM((SAMPLES, 2, CPAD, COLS), BF16),
            pltpu.VMEM((NLON, 48, COLS), BF16),
            pltpu.VMEM((NLON, 48, COLS), BF16),
            pltpu.VMEM((NLON, 48, COLS), BF16),
            pltpu.VMEM((NLON, 48, COLS), BF16),
            pltpu.VMEM((NLON, 16, 128), BF16),
            pltpu.VMEM((NLON, 16, 128), BF16),
            pltpu.VMEM((2, CPAD, 128), F32),
            dma((3 + SAMPLES,)), dma((ROWS,)),
            dma((2,)), dma((2,)), dma((SAMPLES,)), dma((SAMPLES,)), dma((SAMPLES,)), dma((SAMPLES,)), dma((6,)), dma((6,)),
            dma((NLON,)), dma((NLON,)), dma((NLON,)), dma((NLON,)), dma((NLON,)), dma((NLON,)),
        ],
        compiler_params=pltpu.CompilerParams(collective_id=0, has_side_effects=True, vmem_limit_bytes=LIMIT),
    )(state, mask, fold, k1, b1, k2, b2)


CHANNELS = 128
AHEAD = 8
CHUNKS = [(s, c) for s in range(SAMPLES) for c in range(HID // CHANNELS)]


def order_kernel(y_hbm, edge_ref, out_hbm, y_ref, out_ref, load_sem, store_sem):
    loads, stores = [], []
    for n, (s, c) in enumerate(CHUNKS):
        part = pl.ds(c * CHANNELS, CHANNELS)
        loads.append(pltpu.make_async_copy(y_hbm.at[s, :, part], y_ref.at[n], load_sem.at[n]))
        stores.append(pltpu.make_async_copy(out_ref.at[n], out_hbm.at[s, part], store_sem.at[n]))
    for load in loads[:AHEAD]:
        load.start()
    lane = lanes_of((CHANNELS, 128))
    at_first = jnp.where(lane < 2, 1.0, 0.0).astype(BF16)
    at_last = jnp.where(lane >= 126, 1.0, 0.0).astype(BF16)
    for n, (s, c) in enumerate(CHUNKS):
        cut = slice(c * CHANNELS, (c + 1) * CHANNELS)
        first, last = edge_ref[0, cut], edge_ref[1, cut]
        loads[n].wait()
        if n + AHEAD < len(loads):
            loads[n + AHEAD].start()
        rows = []
        for r in range(ROWS):
            at = 8 * r + 2 * s
            low = at_first * (pltpu.roll(first, 128 - at, 1) if at else first)
            high = at_last * pltpu.roll(last, 126 - at, 1)
            rows.append(jnp.concatenate([y_ref[n, r, :, :128] + low, y_ref[n, r, :, 128:] + high], 1))
        out_ref[n] = jnp.swapaxes(jnp.stack(rows), 0, 1)
        stores[n].start()
    for store in stores:
        store.wait()


def order(y, edges):
    return pl.pallas_call(
        order_kernel,
        out_shape=jax.ShapeDtypeStruct((SAMPLES, HID, ROWS, COLS), BF16),
        in_specs=[HBM, VMEM],
        out_specs=HBM,
        scratch_shapes=[
            pltpu.VMEM((len(CHUNKS), ROWS, CHANNELS, COLS), BF16),
            pltpu.VMEM((len(CHUNKS), CHANNELS, ROWS, COLS), BF16),
            pltpu.SemaphoreType.DMA((len(CHUNKS),)),
            pltpu.SemaphoreType.DMA((len(CHUNKS),)),
        ],
        compiler_params=pltpu.CompilerParams(vmem_limit_bytes=LIMIT),
    )(y, edges)


def on_device(state, mask, fold, first_kernel, first_bias, second_kernel, second_bias):
    y, edges = main(state, mask, fold, jnp.transpose(first_kernel, (0, 2, 1)), first_bias[None], second_kernel, second_bias[None])
    return order(y, edges)


def solution(mesh):
    return jax.shard_map(
        on_device,
        mesh=mesh,
        in_specs=(P(None, None, "lat", "lon"), P(None, "lat", "lon"), P("lon"), P(), P(), P(), P()),
        out_specs=P(None, None, "lat", "lon"),
        check_vma=False,
    )
```
